32 devices in a mesh: dp: 16 (over z, y, core), fsdp: 2 (over x).
Axes of the slice: x: 2, y: 2, z: 4, core: 2. Of those that a mesh axis runs over, the one named last changes fastest.
Arguments:
- inputs: bfloat16 [32768, 512], P(('dp', 'fsdp')), may hold values from -6 to 6
- documents: int32 [32, 1024], P(('dp', 'fsdp')), may hold values from 0 to 7, never falling along the last dimension, each value on 1 to 512 neighbouring positions
- first_gain: bfloat16 [512], P(('dp', 'fsdp')), may hold values from 0.5 to 1.5
- first_shift: bfloat16 [512], P(('dp', 'fsdp')), may hold values from -1.75 to 1.75
- attend_weight: bfloat16 [512, 1536], P(('dp', 'fsdp')), may hold values from -0.25 to 0.25
- position_table: bfloat16 [256], P(('dp', 'fsdp')), may hold values from -6 to 6
- output_weight: bfloat16 [512, 512], P(('dp', 'fsdp')), may hold values from -1.5 to 1.5
- output_shift: bfloat16 [512], P(('dp', 'fsdp')), may hold values from -1.75 to 1.75
- second_gain: bfloat16 [512], P(('dp', 'fsdp')), may hold values from 0.5 to 1.5
- second_shift: bfloat16 [512], P(('dp', 'fsdp')), may hold values from -1.75 to 1.75
- expand_weight: bfloat16 [512, 2048], P(('dp', 'fsdp')), may hold values from -0.25 to 0.25
- expand_shift: bfloat16 [2048], P(('dp', 'fsdp')), may hold values from -1.75 to 1.75
- reduce_weight: bfloat16 [2048, 512], P(('dp', 'fsdp')), may hold values from -0.125 to 0.125
- reduce_shift: bfloat16 [512], P(('dp', 'fsdp')), may hold values from -1.75 to 1.75
- cotangent: bfloat16 [32768, 512], P(('dp', 'fsdp')), may hold values from -6 to 6
Outputs:
- output: bfloat16 [32768, 512], P(('dp', 'fsdp'))
- input_grad: float32 [32768, 512], P(('dp', 'fsdp'))
- first_gain_grad: float32 [512], P(('dp', 'fsdp'))
- first_shift_grad: float32 [512], P(('dp', 'fsdp'))
- attend_weight_grad: float32 [512, 1536], P(('dp', 'fsdp'))
- position_table_grad: float32 [256], P(('dp', 'fsdp'))
- output_weight_grad: float32 [512, 512], P(('dp', 'fsdp'))
- output_shift_grad: float32 [512], P(('dp', 'fsdp'))
- second_gain_grad: float32 [512], P(('dp', 'fsdp'))
- second_shift_grad: float32 [512], P(('dp', 'fsdp'))
- expand_weight_grad: float32 [512, 2048], P(('dp', 'fsdp'))
- expand_shift_grad: float32 [2048], P(('dp', 'fsdp'))
- reduce_weight_grad: float32 [2048, 512], P(('dp', 'fsdp'))
- reduce_shift_grad: float32 [512], P(('dp', 'fsdp'))
The draws below stay inside these ranges and needn't reach their ends.
Inputs may be any that keep to these rules, and one draw needn't show every extreme that they name: `documents`: in each row the document numbers never fall, every number up to 7 appears, no document has more than 512 tokens and one in each row has exactly that many.
All inputs are finite; a program needn't handle non-finite values.
Results may differ from the reference program's by a relative error of at most 0.02.
Values may be sent and summed in bfloat16 or wider, within the bound.
A program may use at most 256 MiB of HBM per device.

```python
import math
import jax
import jax.numpy as jnp
import numpy as np
from jax import lax

D = 512
HEADS = 8
FF = 2048
HEAD_DIM = 64
BUCKETS = 32
SEQ_LEN = 1024
DOCS = 8
SEQS = 32
TOKENS = 32768


def levels(stream_key, extent, shards, low, high):
    def one(dim, shards_of):
        heights = jax.random.uniform(jax.random.fold_in(jax.random.fold_in(stream_key, 6), dim), (shards_of,), jnp.float32, low / len(shards), high / len(shards))
        return jnp.repeat(jnp.exp(heights), extent[dim] // shards_of).reshape((-1,) + (1,) * (len(extent) - dim - 1))

    loudness = one(*shards[0])
    for cut in shards[1:]:
        loudness = loudness * one(*cut)
    return loudness


def profile(count, total, bound, slope):
    weights = [(1 << 20) // math.isqrt(grade ** slope) + 1 for grade in range(2, count + 1)]
    spare, given = total - bound - (count - 1), [1] * (count - 1)
    while spare > 0:
        movable = [i for i in range(count - 1) if given[i] < bound]
        whole, remaining = sum([weights[i] for i in movable]), spare
        for i in movable:
            extra = min(bound - given[i], max(1, remaining * weights[i] // whole), spare)
            given[i] = given[i] + extra
            spare = spare - extra
    return np.array([bound] + given)


def ragged(own_key, count, total, limit, lean):
    if count == 2:
        one = jax.random.randint(own_key, (), max(1, total - limit), min(limit, total - 1) + 1)
        return jnp.stack([one, total - one])
    lengths = jnp.asarray(profile(count, total, limit, lean), jnp.int32)
    couples = (count - 1) // 2
    giver, taker = lengths[1:1 + 2 * couples:2], lengths[2:2 + 2 * couples:2]
    room = jnp.minimum(giver - 1, limit - taker)
    passed = jax.random.randint(jax.random.fold_in(own_key, 1), (couples,), 0, 1 << 20) % (room + 1)
    lengths = lengths.at[1:1 + 2 * couples:2].set(giver - passed).at[2:2 + 2 * couples:2].set(taker + passed)
    return lengths[jax.random.permutation(jax.random.fold_in(own_key, 2), count)]


def normal_values(stream_key, shape, scale, limit, cuts=(), kind=jnp.bfloat16):
    factor_of = levels(stream_key, shape, cuts, -0.22, 0.18) if cuts else 1.0
    array = jax.random.normal(stream_key, shape, jnp.float32) * scale * factor_of
    return jnp.minimum(jnp.maximum(array, -limit), limit).astype(kind)


def setup_inputs(seed: int = 0) -> dict:
    keys = jax.random.split(jax.random.key(seed), 16)
    inputs = normal_values(keys[0], (TOKENS, D), 1.0, 6.0, ((0, 32),))
    documents = jax.vmap(lambda own: jnp.searchsorted(jnp.cumsum(ragged(own, DOCS, SEQ_LEN, SEQ_LEN // 2, 0)), jnp.arange(SEQ_LEN), side="right"))(jax.random.split(keys[1], SEQS)).reshape((SEQS, SEQ_LEN)).astype(jnp.int32)
    first_gain = jnp.clip(1.0 + 0.1 * jax.random.normal(keys[2], (D,), jnp.float32), 0.5, 1.5).astype(jnp.bfloat16)
    first_shift = normal_values(keys[3], (D,), 0.3, 1.75, ((0, 32),))
    attend_weight = normal_values(keys[4], (D, 3 * D), D ** -0.5, 0.25, ((0, 32),))
    position_table = normal_values(keys[5], (HEADS * BUCKETS,), 1.0, 6.0, ((0, 32),))
    output_weight = normal_values(keys[6], (D, D), (D // 32) ** -0.5, 1.5, ((0, 32),))
    output_shift = normal_values(keys[7], (D,), 0.3, 1.75, ((0, 32),))
    second_gain = jnp.clip(1.0 + 0.1 * jax.random.normal(keys[8], (D,), jnp.float32), 0.5, 1.5).astype(jnp.bfloat16)
    second_shift = normal_values(keys[9], (D,), 0.3, 1.75, ((0, 32),))
    expand_weight = normal_values(keys[10], (D, FF), D ** -0.5, 0.25, ((0, 32),))
    expand_shift = normal_values(keys[11], (FF,), 0.3, 1.75, ((0, 32),))
    reduce_weight = normal_values(keys[12], (FF, D), FF ** -0.5, 0.125, ((0, 32),))
    reduce_shift = normal_values(keys[13], (D,), 0.3, 1.75, ((0, 32),))
    cotangent = normal_values(keys[14], (TOKENS, D), 1.0, 6.0, ((0, 32),))
    return dict(inputs=inputs, documents=documents, first_gain=first_gain, first_shift=first_shift, attend_weight=attend_weight, position_table=position_table, output_weight=output_weight, output_shift=output_shift, second_gain=second_gain, second_shift=second_shift, expand_weight=expand_weight, expand_shift=expand_shift, reduce_weight=reduce_weight, reduce_shift=reduce_shift, cotangent=cotangent)


eps = 1e-05
far_reach = 128

@jax.custom_vjp
def low(v):
    return lax.optimization_barrier(v.astype(jnp.bfloat16)).astype(jnp.float32)

@jax.custom_vjp
def low_back(v):
    return v

def low_keep(v):
    return (low(v), None)

def low_pass(kept, grad):
    return (grad,)

def back_keep(v):
    return (v, None)

def back_low(kept, grad):
    return (low(grad),)
low.defvjp(low_keep, low_pass)
low_back.defvjp(back_keep, back_low)

def bucket_of(distance):
    exact_count = BUCKETS // 2
    counted = jnp.minimum(distance, exact_count)
    for level_j in range(1, exact_count):
        border = int(exact_count * (far_reach / exact_count) ** (level_j / exact_count))
        counted = counted + (distance >= border).astype(jnp.int32)
    return counted

def normalize(values, norm_gain, norm_shift):
    center = values - lax.optimization_barrier(jnp.mean(values, axis=-1, keepdims=True))
    spread = lax.optimization_barrier(jnp.mean(center * center, axis=-1, keepdims=True))
    return center * lax.rsqrt(spread + eps) * norm_gain + norm_shift

def layer(layer_in, doc_ids, params):
    first_gain, first_shift, attend_weight, position_table, output_weight, output_shift, second_gain, second_shift, expand_weight, expand_shift, reduce_weight, reduce_shift = params
    highest = lax.Precision.HIGHEST
    length = layer_in.shape[0]
    normed_a = low(normalize(layer_in, first_gain, first_shift))
    projected = low_back(low(jnp.dot(normed_a, attend_weight, precision=highest)))
    projected = projected.reshape(length, 3, HEADS, HEAD_DIM)
    raw = jnp.einsum('qhd,khd->hqk', projected[:, 0], projected[:, 1], precision=highest) * HEAD_DIM ** (-0.5)
    query_pos = jnp.arange(length, dtype=jnp.int32)[:, None]
    key_pos = jnp.arange(length, dtype=jnp.int32)[None, :]
    distance = query_pos - key_pos
    buckets = bucket_of(jnp.maximum(distance, 0))
    bias_table = position_table.reshape(HEADS, BUCKETS)
    scores = low_back(raw + bias_table[:, buckets])
    allowed = jnp.logical_and(distance >= 0, doc_ids[:, None] == doc_ids[None, :])
    soft_weights = low(jax.nn.softmax(jnp.where(allowed[None], scores, -1e+30), axis=-1))
    attended = jnp.einsum('hqk,khd->qhd', soft_weights, projected[:, 2], precision=highest).reshape(length, D)
    attended = low_back(low(attended))
    branch = low_back(jnp.dot(attended, output_weight, precision=highest) + output_shift)
    residual = layer_in + branch
    normed_f = low(normalize(residual, second_gain, second_shift))
    hidden = low_back(jnp.dot(normed_f, expand_weight, precision=highest) + expand_shift)
    active = low(jax.nn.gelu(hidden, approximate=False))
    return residual + low_back(jnp.dot(active, reduce_weight, precision=highest) + reduce_shift)

def reference(inputs, documents, first_gain, first_shift, attend_weight, position_table, output_weight, output_shift, second_gain, second_shift, expand_weight, expand_shift, reduce_weight, reduce_shift, cotangent):
    params = tuple((item.astype(jnp.float32) for item in (first_gain, first_shift, attend_weight, position_table, output_weight, output_shift, second_gain, second_shift, expand_weight, expand_shift, reduce_weight, reduce_shift)))
    sequences = inputs.astype(jnp.float32).reshape(-1, SEQ_LEN, D)

    def whole(seq_in, weights):

        def one_seq(paired):
            return layer(paired[0], paired[1], weights)
        return lax.map(jax.checkpoint(one_seq), (seq_in, documents))
    result, pullback = jax.vjp(whole, sequences, params)
    grad_seq, grads = pullback(cotangent.astype(jnp.float32).reshape(-1, SEQ_LEN, D))
    return (result.reshape(-1, D).astype(jnp.bfloat16), grad_seq.reshape(-1, D), grads[0], grads[1], grads[2], grads[3], grads[4], grads[5], grads[6], grads[7], grads[8], grads[9], grads[10], grads[11])
```

```python
import types

import jax
import jax.numpy as jnp
from jax import lax
from jax.experimental import pallas as pl
from jax.experimental.pallas import tpu as pltpu
from jax.sharding import PartitionSpec as P

D = 512
HEADS = 8
HEAD_DIM = 64
BUCKETS = 32
LONGEST = 512
TILE = 128
PAIRS = HEADS // 2
NEG = -1e30
eps = 1e-05
far_reach = 128

bf16 = jnp.bfloat16
f32 = jnp.float32
AXES = ("dp", "fsdp")


def iota(shape, dim):
    return lax.broadcasted_iota(jnp.int32, shape, dim)


def bucket_of(distance):
    exact_count = BUCKETS // 2
    counted = jnp.minimum(distance, exact_count)
    for level_j in range(1, exact_count):
        border = int(exact_count * (far_reach / exact_count) ** (level_j / exact_count))
        counted = counted + (distance >= border).astype(jnp.int32)
    return counted


def dot_nn(a, b):
    return lax.dot_general(a, b, (((1,), (0,)), ((), ())), preferred_element_type=f32)


def dot_nt(a, b):
    return lax.dot_general(a, b, (((1,), (1,)), ((), ())), preferred_element_type=f32)


def dot_tn(a, b):
    return lax.dot_general(a, b, (((0,), (0,)), ((), ())), preferred_element_type=f32)


def onehot(mask):
    return jnp.where(mask, 1.0, 0.0).astype(bf16)


def standardize(v):
    center = v - jnp.mean(v, axis=-1, keepdims=True)
    spread = jnp.mean(center * center, axis=-1, keepdims=True)
    rstd = lax.rsqrt(spread + eps)
    return center * rstd, rstd


def standardize_back(dx, xh, rstd):
    return rstd * (
        dx
        - jnp.mean(dx, axis=-1, keepdims=True)
        - xh * jnp.mean(dx * xh, axis=-1, keepdims=True)
    )


def gelu_parts(h):
    t = 1.0 / (1.0 + (0.3275911 * 0.7071067811865476) * jnp.abs(h))
    e = jnp.exp(-0.5 * h * h)
    poly = t * (
        0.127414796
        + t * (-0.142248368 + t * (0.7107068705 + t * (-0.7265760135 + t * 0.5307027145)))
    )
    tail = poly * e
    phi = jnp.where(h >= 0, 1.0 - tail, tail)
    return h * phi, phi + h * (e * 0.3989422804014327)


def split_heads(t):
    top = iota(t.shape, 0) < HEAD_DIM
    zero = jnp.zeros_like(t)
    return jnp.concatenate([jnp.where(top, t, zero), jnp.where(top, zero, t)], axis=1)


def join_heads(t):
    n = t.shape[1] // 2
    return jnp.concatenate([t[:HEAD_DIM, :n], t[HEAD_DIM:, n:]], axis=0)


def unpack_small(r, n):
    packed = r.A[:, 4 * D :]
    rows, lanes = iota((16 * n, D), 0), iota((16 * n, D), 1)
    per = D // n
    rep = onehot(iota((128, D), 1) % per == iota((128, D), 0))
    wide = dot_nn(packed, rep)
    wide = jnp.where(lanes // per == rows // 16, wide, 0.0)
    r.sm[...] = jnp.sum(wide.reshape(n, 16, D), axis=0)
    ff = r.es.shape[1]
    per = ff // n
    pick = onehot(iota((n, 16 * n), 1) == 16 * iota((n, 16 * n), 0) + 6)
    rep = onehot(iota((128, ff), 1) % per == iota((128, ff), 0))
    wide = dot_nn(dot_nn(pick, packed).astype(bf16), rep)
    wide = jnp.where(iota((n, ff), 1) // per == iota((n, ff), 0), wide, 0.0)
    r.es[...] = jnp.broadcast_to(jnp.sum(wide, axis=0, keepdims=True), r.es.shape)
    per = HEADS * BUCKETS // n
    group = BUCKETS // per
    pick = onehot(iota((n, 16 * n), 1) == 16 * iota((n, 16 * n), 0) + 7)
    bucket = bucket_of(iota((128, 256), 1))
    rep = onehot(bucket % per == iota((128, 256), 0))
    wide = dot_nn(dot_nn(pick, packed).astype(bf16), rep)
    bucket = bucket_of(iota((n, 256), 1))
    wide = jnp.where(bucket // per == iota((n, 256), 0) % group, wide, 0.0).astype(bf16)
    gather = onehot(iota((HEADS, n), 1) // group == iota((HEADS, n), 0))
    r.bd[...] = dot_nn(gather, wide)


def pack_small_grads(r, n):
    rows, lanes = iota((16 * n, D), 0), iota((16 * n, D), 1)
    per = D // n
    wide = jnp.broadcast_to(r.smg[...][None], (n, 16, D)).reshape(16 * n, D)
    wide = jnp.where(lanes // per == rows // 16, wide, 0.0).astype(bf16)
    rep = onehot(iota((128, D), 1) % per == iota((128, D), 0))
    packed = dot_nt(wide, rep)
    ff = r.esg.shape[1]
    per = ff // n
    rep = onehot(iota((128, ff), 1) % per == iota((128, ff), 0))
    wide = jnp.broadcast_to(r.esg[0:1, :], (n, ff))
    wide = jnp.where(iota((n, ff), 1) // per == iota((n, ff), 0), wide, 0.0).astype(bf16)
    part = dot_nt(wide, rep).astype(bf16)
    place = onehot(iota((16 * n, n), 0) == 16 * iota((16 * n, n), 1) + 6)
    packed = packed + dot_nn(place, part)
    per = HEADS * BUCKETS // n
    group = BUCKETS // per
    spread = onehot(iota((n, HEADS), 0) // group == iota((n, HEADS), 1))
    wide = dot_nn(spread, r.tg[...].astype(bf16))
    wide = jnp.where(iota((n, 128), 1) // per == iota((n, 128), 0) % group, wide, 0.0)
    rep = onehot(iota((128, 128), 1) % per == iota((128, 128), 0))
    part = dot_nt(wide.astype(bf16), rep).astype(bf16)
    place = onehot(iota((16 * n, n), 0) == 16 * iota((16 * n, n), 1) + 7)
    return packed + dot_nn(place, part)


def norm_first(r):
    def rows(i, c):
        s = pl.ds(pl.multiple_of(i * 256, 256), 256)
        xh, _ = standardize(r.x[s, :].astype(f32))
        r.na[s, :] = (xh * r.sm[0:1, :] + r.sm[1:2, :]).astype(bf16)
        return c

    lax.fori_loop(0, r.x.shape[0] // 256, rows, 0)


def masks(r):
    length = r.docs.shape[1]
    same = iota((128, length), 0) == r.docs[...]
    r.kd[...] = jnp.where(same, 1.0, 0.0).T.astype(bf16)
    differ = jnp.logical_and(iota((128, length), 0) < 8, jnp.logical_not(same))
    r.qd[...] = jnp.where(differ, NEG, 0.0).astype(bf16)


def near_bias(r):
    for h in range(HEADS):
        by_dist = r.bd[h : h + 1, :]
        by_dist = by_dist - by_dist[:, 255:256]
        line = jnp.concatenate([jnp.full((1, TILE), NEG, f32), by_dist], axis=1)
        line = jnp.broadcast_to(line, (TILE, 3 * TILE))
        line = pltpu.roll(line, 0, 1, stride=1, stride_axis=0)
        half = slice((h % 2) * TILE, (h % 2 + 1) * TILE)
        r.near[h // 2, 0:TILE, half] = line[:, 2 * TILE :]
        r.near[h // 2, TILE:, half] = line[:, TILE : 2 * TILE]


def project(r):
    def rows(i, c):
        s = pl.ds(pl.multiple_of(i * 256, 256), 256)
        out = dot_nn(r.na[s, :], r.A[:, 0 : 3 * D])
        q = (out[:, :D].astype(bf16) * bf16(HEAD_DIM**-0.5)).T
        k = out[:, D : 2 * D].astype(bf16)
        v = out[:, 2 * D :].astype(bf16)
        for p in range(PAIRS):
            lanes = slice(p * 128, (p + 1) * 128)
            r.qt[p, :, s] = q[lanes, :]
            r.k[p, s, :] = k[:, lanes]
            r.v[p, s, :] = v[:, lanes]
        return c

    lax.fori_loop(0, r.x.shape[0] // 256, rows, 0)


def bands(length):
    first = 0
    for b in range(length // TILE):
        low = max(0, b - LONGEST // TILE)
        count = (b + 1 - low) * TILE
        yield b, slice(low * TILE, (b + 1) * TILE), slice(b * TILE, (b + 1) * TILE), first, count
        first += count


def band_rows(length):
    return sum(count for _, _, _, _, count in bands(length))


def attend_forward(r, p):
    near = r.near[p]
    lanes = pl.ds(pl.multiple_of(p * 128, 128), 128)
    for b, ks, qs, first, count in bands(r.x.shape[0]):
        qd = r.qd[:, qs]
        rhs = jnp.concatenate(
            [split_heads(r.qt[p, :, qs]), jnp.concatenate([qd, qd], axis=1)], axis=0
        )
        lhs = jnp.concatenate([r.k[p, ks, :], r.kd[ks, :]], axis=1)
        st = dot_nn(lhs, rhs)
        if count > 2 * TILE:
            st = jnp.concatenate([st[: count - 2 * TILE], st[count - 2 * TILE :] + near], axis=0)
        else:
            st = st + near[2 * TILE - count :]
        lifted = jnp.exp(st - jnp.max(st, axis=0, keepdims=True))
        inverse = 1.0 / jnp.sum(lifted, axis=0, keepdims=True)
        weights = lifted.astype(bf16)
        r.P[p, first : first + count, :] = weights
        r.inv[p, b : b + 1, :] = inverse
        ot = join_heads(dot_tn(r.v[p, ks, :], weights) * inverse)
        r.ot[p, :, qs] = ot
        r.att[qs, lanes] = ot.T.astype(bf16)


def attend_backward(r, p):
    length = r.x.shape[0]
    r.dk[...] = jnp.zeros_like(r.dk)
    r.dv[...] = jnp.zeros_like(r.dv)
    r.acc[...] = jnp.zeros_like(r.acc)
    lanes = [pl.ds(pl.multiple_of(p * 128 + part * D, 128), 128) for part in range(3)]
    top = iota((128, TILE), 0) < HEAD_DIM
    for b, ks, qs, first, count in bands(length):
        inverse = r.inv[p, b : b + 1, :]
        scale = jnp.where(top, inverse[:, :TILE], inverse[:, TILE:])
        dot_ = (r.dot[p, :, qs] * scale).astype(bf16)
        prod = dot_.astype(f32) * r.ot[p, :, qs]
        delta = jnp.concatenate(
            [
                jnp.sum(prod[:HEAD_DIM], axis=0, keepdims=True),
                jnp.sum(prod[HEAD_DIM:], axis=0, keepdims=True),
            ],
            axis=1,
        )
        dcat = split_heads(dot_)
        weights = r.P[p, first : first + count, :]
        ds = weights.astype(f32) * (dot_nn(r.v[p, ks, :], dcat) - delta)
        dsb = ds.astype(bf16)
        if count >= 2 * TILE:
            r.acc[...] += ds[count - 2 * TILE :]
        else:
            r.acc[TILE:, :] += ds
        r.dv[ks, :] += dot_nt(weights, dcat)
        r.dk[ks, :] += dot_nt(dsb, split_heads(r.qt[p, :, qs]))
        dqt = join_heads(dot_tn(r.k[p, ks, :], dsb)) * HEAD_DIM**-0.5
        r.dproj[qs, lanes[0]] = dqt.T.astype(bf16)
    r.dproj[:, lanes[1]] = r.dk[...].astype(bf16)
    r.dproj[:, lanes[2]] = r.dv[...].astype(bf16)
    zero = jnp.zeros((TILE, TILE), f32)
    rows = iota((TILE, 3 * TILE), 0)
    for h in range(2):
        half = slice(h * TILE, (h + 1) * TILE)
        line = jnp.concatenate([zero, r.acc[TILE:, half], r.acc[:TILE, half]], axis=1)
        for bit in range(7):
            rolled = pltpu.roll(line, 3 * TILE - (1 << bit), 1)
            line = jnp.where((rows >> bit) & 1 == 1, rolled, line)
        r.lines[pl.ds(2 * p + h, 1), :] = jnp.sum(line, axis=0, keepdims=True)


def table_grad(r):
    by_dist = r.lines[:, TILE:]
    dist = iota((2 * TILE, 128), 0)
    near = jnp.logical_and(bucket_of(dist) == iota((2 * TILE, 128), 1), dist < 2 * TILE)
    near = jnp.logical_and(near, iota((2 * TILE, 128), 1) < BUCKETS - 1)
    counted = lax.dot_general(
        by_dist,
        jnp.where(near, 1.0, 0.0),
        (((1,), (0,)), ((), ())),
        precision=lax.Precision.HIGHEST,
        preferred_element_type=f32,
    )
    rest = -jnp.sum(counted, axis=1, keepdims=True)
    r.tg[...] = jnp.where(iota((HEADS, 128), 1) == BUCKETS - 1, rest, counted)


def middle(r):
    ff = r.es.shape[1]
    wide = 512
    r.smg[...] = jnp.zeros_like(r.smg)
    r.esg[...] = jnp.zeros_like(r.esg)

    def rows(i, c):
        s = pl.ds(pl.multiple_of(i * 256, 256), 256)
        residual = (
            r.x[s, :].astype(f32) + dot_nn(r.att[s, :], r.A[:, 3 * D : 4 * D]) + r.sm[2:3, :]
        )
        xh, rstd = standardize(residual)
        nf = (xh * r.sm[3:4, :] + r.sm[4:5, :]).astype(bf16)
        r.nf[s, :] = nf
        g = r.g[s, :]
        branch = jnp.zeros((256, D), f32)
        gnf = jnp.zeros((256, D), f32)
        for f in range(ff // wide):
            cols = slice(f * wide, (f + 1) * wide)
            hidden = dot_nn(nf, r.W1[:, cols]) + r.es[0:1, cols]
            active, slope = gelu_parts(hidden)
            active = active.astype(bf16)
            r.act[s, cols] = active
            gh = dot_nt(g, r.W2[cols, :]) * slope
            r.esg[0:1, cols] += jnp.sum(gh, axis=0, keepdims=True)
            gh = gh.astype(bf16)
            r.gh[s, cols] = gh
            branch = branch + dot_nn(active, r.W2[cols, :])
            gnf = gnf + dot_nt(gh, r.W1[:, cols])
        r.out[s, :] = (residual + branch + r.sm[5:6, :]).astype(bf16)
        gf = g.astype(f32)
        grad = gf + standardize_back(gnf * r.sm[3:4, :], xh, rstd)
        r.gres[s, :] = grad
        gb = grad.astype(bf16)
        r.gb[s, :] = gb
        r.smg[2:3, :] += jnp.sum(gb.astype(f32), axis=0, keepdims=True)
        r.smg[3:4, :] += jnp.sum(gnf * xh, axis=0, keepdims=True)
        r.smg[4:5, :] += jnp.sum(gnf, axis=0, keepdims=True)
        r.smg[5:6, :] += jnp.sum(gf, axis=0, keepdims=True)
        dot_ = dot_nt(gb, r.A[:, 3 * D : 4 * D]).T
        for p in range(PAIRS):
            r.dot[p, :, s] = dot_[p * 128 : (p + 1) * 128, :]
        return c

    lax.fori_loop(0, r.x.shape[0] // 256, rows, 0)


def last(r):
    def rows(i, c):
        s = pl.ds(pl.multiple_of(i * 256, 256), 256)
        gna = dot_nt(r.dproj[s, :], r.A[:, 0 : 3 * D])
        xh, rstd = standardize(r.x[s, :].astype(f32))
        r.igrad[s, :] = r.gres[s, :] + standardize_back(gna * r.sm[0:1, :], xh, rstd)
        r.smg[0:1, :] += jnp.sum(gna * xh, axis=0, keepdims=True)
        r.smg[1:2, :] += jnp.sum(gna, axis=0, keepdims=True)
        return c

    lax.fori_loop(0, r.x.shape[0] // 256, rows, 0)


def weight_grad(left, right, step, put):
    def rows(i, c):
        put(i, dot_tn(left[:, pl.ds(pl.multiple_of(i * step, step), step)], right[...]))
        return c

    lax.fori_loop(0, left.shape[1] // step, rows, 0)


class Place:
    def __init__(self, dp_size, fsdp_size):
        dp, x = lax.axis_index("dp"), lax.axis_index("fsdp")
        self.z, self.y, self.c, self.x = dp // 4, (dp // 2) % 2, dp % 2, x
        self.zs = dp_size // 4

    def zpeer(self, m):
        z = self.z
        return (z, z + 1 - 2 * (z % 2), (z + 2) % 4, 3 - z)[m]

    def index(self, m, t, other=False):
        x = 1 - self.x if t in (1, 3) else self.x
        y = 1 - self.y if t in (2, 3) else self.y
        c = 1 - self.c if other else self.c
        return ((self.zpeer(m) * 2 + y) * 2 + c) * 2 + x

    def inner(self, t, other=False):
        x = 1 - self.x if t in (1, 3) else self.x
        y = 1 - self.y if t in (2, 3) else self.y
        c = 1 - self.c if other else self.c
        return (y * 2 + c) * 2 + x

    def device(self, m=0, t=0, other=False):
        x = 1 - self.x if t in (1, 3) else self.x
        y = 1 - self.y if t in (2, 3) else self.y
        c = 1 - self.c if other else self.c
        return ((self.zpeer(m) * 2 + y) * 2 + c, x)

    def neighbours(self):
        return [self.device(m=m) for m in (1, 2, 3)] + [
            self.device(t=1),
            self.device(t=2),
            self.device(other=True),
        ]


def enter(place):
    barrier = pltpu.get_barrier_semaphore()
    for peer in place.neighbours():
        pl.semaphore_signal(
            barrier, inc=1, device_id=peer, device_id_type=pl.DeviceIdType.MESH
        )
    pl.semaphore_wait(barrier, 6)


GATHER_SEMS = 35
Z0, X0, Y0, OA0, OB0, S0 = -1, 3, 7, 11, 15, 19


class Gather:
    def __init__(self, place, whole, rho, half, send, recv):
        self.place, self.whole, self.rho, self.half = place, whole, rho, half
        self.send, self.recv = send, recv
        self.started = []

    def view(self, shard, part=None):
        rows = pl.ds(pl.multiple_of(shard * self.rho, 16), self.rho)
        if part is None:
            return self.whole.at[rows, :]
        cols = slice(0, self.half) if part == 0 else slice(self.half, self.whole.shape[1])
        return self.whole.at[rows, cols]

    def copy(self, shard, sem, device, part=None):
        ref = self.view(shard, part)
        return pltpu.make_async_remote_copy(
            src_ref=ref,
            dst_ref=ref,
            send_sem=self.send.at[sem],
            recv_sem=self.recv.at[sem],
            device_id=device,
            device_id_type=pl.DeviceIdType.MESH,
        )

    def start(self, shard, sem, device, part=None):
        self.copy(shard, sem, device, part).start()
        self.started.append((sem, part))

    def arrive(self, shard, sem, part=None):
        self.copy(shard, sem, self.place.device(other=True), part).wait_recv()

    def spread(self, m):
        at = self.place
        shard = at.index(m, 0)
        self.start(shard, X0 + m, at.device(t=1))
        self.start(shard, Y0 + m, at.device(t=2))
        self.start(shard, S0 + m, at.device(other=True))

    def first(self):
        at = self.place
        for m in (1, 2, 3):
            self.start(at.index(0, 0), Z0 + m, at.device(m=m))
        self.spread(0)

    def second(self, m):
        self.arrive(self.place.index(m, 0), Z0 + m)
        self.spread(m)

    def third(self, m):
        at = self.place
        shard = at.index(m, 1)
        self.arrive(shard, X0 + m)
        self.start(shard, OA0 + m, at.device(t=2), 0)
        self.start(shard, S0 + 4 + m, at.device(other=True))
        shard = at.index(m, 2)
        self.arrive(shard, Y0 + m)
        self.start(shard, OB0 + m, at.device(t=1), 1)
        self.start(shard, S0 + 8 + m, at.device(other=True))

    def fourth(self, m):
        at = self.place
        shard = at.index(m, 3)
        self.arrive(shard, OA0 + m, 0)
        self.arrive(shard, OB0 + m, 1)
        self.start(shard, S0 + 12 + m, at.device(other=True))

    def finish(self):
        for t in range(4):
            for m in range(4):
                self.arrive(self.place.index(m, t, other=True), S0 + 4 * t + m)

    def drain(self):
        at = self.place
        for sem, part in self.started:
            self.copy(at.index(0, 0), sem, at.device(other=True), part).wait_send()


SCATTER_SEMS = 11


class Scatter:
    def __init__(self, place, full, bufs, out, half, send, recv):
        self.place, self.full, self.out, self.half = place, full, out, half
        self.sib, self.ra, self.rb, self.rx, self.ry, self.rz = bufs
        self.send, self.recv = send, recv
        self.started = []

    def copy(self, src, dst, sem, device):
        return pltpu.make_async_remote_copy(
            src_ref=src,
            dst_ref=dst,
            send_sem=self.send.at[sem],
            recv_sem=self.recv.at[sem],
            device_id=device,
            device_id_type=pl.DeviceIdType.MESH,
        )

    def start(self, src, dst, sem, device):
        self.copy(src, dst, sem, device).start()
        self.started.append(sem)

    def arrive(self, dst, sem):
        self.copy(dst, dst, sem, self.place.device(other=True)).wait_recv()

    def first(self):
        at = self.place
        for t in (3, 1, 2, 0):
            self.start(
                self.full.at[:, at.inner(t, other=True)], self.sib.at[t], t, at.device(other=True)
            )

    def merge(self, t):
        self.arrive(self.sib.at[t], t)
        self.sib[t] += self.full[:, self.place.inner(t)]

    def second(self):
        at = self.place
        self.merge(3)
        self.start(self.sib.at[3, :, :, : self.half], self.ra, 4, at.device(t=1))
        self.start(self.sib.at[3, :, :, self.half :], self.rb, 5, at.device(t=2))

    def third(self):
        at = self.place
        self.merge(1)
        self.merge(2)
        self.arrive(self.rb, 5)
        self.sib[1, :, :, self.half :] += self.rb[...]
        self.start(self.sib.at[1], self.rx, 6, at.device(t=1))
        self.arrive(self.ra, 4)
        self.sib[2, :, :, : self.half] += self.ra[...]
        self.start(self.sib.at[2], self.ry, 7, at.device(t=2))

    def fourth(self):
        at = self.place
        self.merge(0)
        self.arrive(self.rx, 6)
        self.arrive(self.ry, 7)
        self.sib[0] += (self.rx[...].astype(f32) + self.ry[...].astype(f32)).astype(bf16)
        for m in (1, 2, 3):
            self.start(self.sib.at[0, at.zpeer(m)], self.rz.at[m - 1], 7 + m, at.device(m=m))

    def fifth(self):
        total = self.sib[0, self.place.z].astype(f32)
        for m in (1, 2, 3):
            self.arrive(self.rz.at[m - 1], 7 + m)
            total = total + self.rz[m - 1].astype(f32)
        self.out[...] = total

    def drain(self):
        for sem in self.started:
            if sem < 4:
                dst = self.sib.at[sem]
            elif sem < 8:
                dst = (self.ra, self.rb, self.rx, self.ry)[sem - 4]
            else:
                dst = self.rz.at[sem - 8]
            self.copy(dst, dst, sem, self.place.device(other=True)).wait_send()


def scatter_bufs(rho, cols, half):
    return [
        pltpu.VMEM((4, 4, rho, cols), bf16),
        pltpu.VMEM((4, rho, half), bf16),
        pltpu.VMEM((4, rho, cols - half), bf16),
        pltpu.VMEM((4, rho, cols), bf16),
        pltpu.VMEM((4, rho, cols), bf16),
        pltpu.VMEM((3, rho, cols), bf16),
    ]


def work_scratch(length, ff):
    tokens = band_rows(length)
    return dict(
        na=pltpu.VMEM((length, D), bf16),
        kd=pltpu.VMEM((length, 128), bf16),
        qd=pltpu.VMEM((128, length), bf16),
        near=pltpu.VMEM((PAIRS, 2 * TILE, 2 * TILE), f32),
        qt=pltpu.VMEM((PAIRS, 128, length), bf16),
        k=pltpu.VMEM((PAIRS, length, 128), bf16),
        v=pltpu.VMEM((PAIRS, length, 128), bf16),
        P=pltpu.VMEM((PAIRS, tokens, 2 * TILE), bf16),
        inv=pltpu.VMEM((PAIRS, length // TILE, 2 * TILE), f32),
        ot=pltpu.VMEM((PAIRS, 128, length), f32),
        att=pltpu.VMEM((length, D), bf16),
        nf=pltpu.VMEM((length, D), bf16),
        act=pltpu.VMEM((length, ff), bf16),
        gh=pltpu.VMEM((length, ff), bf16),
        gres=pltpu.VMEM((length, D), f32),
        gb=pltpu.VMEM((length, D), bf16),
        dot=pltpu.VMEM((PAIRS, 128, length), f32),
        dk=pltpu.VMEM((length, 128), f32),
        dv=pltpu.VMEM((length, 128), f32),
        acc=pltpu.VMEM((2 * TILE, 2 * TILE), f32),
        lines=pltpu.VMEM((HEADS, 3 * TILE), f32),
        dproj=pltpu.VMEM((length, 3 * D), bf16),
    )


def small_scratch(ff):
    return dict(
        sm=pltpu.VMEM((16, D), f32),
        es=pltpu.VMEM((8, ff), f32),
        bd=pltpu.VMEM((HEADS, 256), f32),
        smg=pltpu.VMEM((16, D), f32),
        esg=pltpu.VMEM((8, ff), f32),
        tg=pltpu.VMEM((HEADS, 128), f32),
    )


PARAMS = dict(vmem_limit_bytes=62 * 1024 * 1024)


def run_kernel(kernel, operands, out_shape, scratch, **params):
    names = list(scratch)
    count = len(operands) + len(out_shape)

    def named(*refs):
        kernel(refs[: len(operands)], refs[len(operands) : count], dict(zip(names, refs[count:])))

    return pl.pallas_call(
        named,
        out_shape=out_shape,
        in_specs=[pl.BlockSpec(memory_space=pltpu.VMEM)] * len(operands),
        out_specs=[pl.BlockSpec(memory_space=pltpu.VMEM)] * len(out_shape),
        scratch_shapes=[scratch[name] for name in names],
        compiler_params=pltpu.CompilerParams(**PARAMS, **params),
    )(*operands)


def whole_layer(x, documents, g, packed, w_a, w_o, w_1, w_2, dp_size, fsdp_size):
    n = dp_size * fsdp_size
    length, ff = x.shape[0], w_1.shape[1]
    ra, r2 = w_1.shape[0], w_2.shape[0]
    cols_a = 4 * D + 128
    work = work_scratch(length, ff)
    small = small_scratch(ff)
    scratch = dict(work, **small)
    scratch.update(
        A=pltpu.VMEM((n * ra, cols_a), bf16),
        W1=pltpu.VMEM((n * ra, ff), bf16),
        W2=pltpu.VMEM((n * r2, D), bf16),
        dA=pltpu.VMEM((4, 8, ra, cols_a), bf16),
        d1=pltpu.VMEM((4, 8, ra, ff), bf16),
        d2=pltpu.VMEM((4, 8, r2, D), bf16),
        gsend=pltpu.SemaphoreType.DMA((3, GATHER_SEMS)),
        grecv=pltpu.SemaphoreType.DMA((3, GATHER_SEMS)),
        ssend=pltpu.SemaphoreType.DMA((3, SCATTER_SEMS)),
        srecv=pltpu.SemaphoreType.DMA((3, SCATTER_SEMS)),
    )
    shapes = [(ra, cols_a, 1024), (ra, ff, ff // 2), (r2, D, D // 2)]
    for i, (rho, cols, half) in enumerate(shapes):
        for j, buf in enumerate(scatter_bufs(rho, cols, half)):
            scratch["buf%d_%d" % (i, j)] = buf

    def kernel(ins, outs, s):
        r = types.SimpleNamespace(**s)
        r.x, r.docs, r.g, own_small, own_a, own_o, own_1, own_2 = ins
        r.out, r.igrad, out_a, out_1, out_2 = outs
        at = Place(dp_size, fsdp_size)
        mine = at.index(0, 0)
        rows_a = pl.ds(pl.multiple_of(mine * ra, 16), ra)
        rows_2 = pl.ds(pl.multiple_of(mine * r2, 16), r2)
        r.A[rows_a, 0 : 3 * D] = own_a[...]
        r.A[rows_a, 3 * D : 4 * D] = own_o[...]
        r.A[rows_a, 4 * D :] = own_small[...]
        r.W1[rows_a, :] = own_1[...]
        r.W2[rows_2, :] = own_2[...]
        enter(at)
        gathers = [
            Gather(at, ref, rho, half, r.gsend.at[i], r.grecv.at[i])
            for i, (ref, (rho, _, half)) in enumerate(zip((r.A, r.W1, r.W2), shapes))
        ]
        ga, g1, g2 = gathers
        ga.first()
        masks(r)
        for m in (1, 2, 3):
            ga.second(m)
        for m in range(4):
            ga.third(m)
        g1.first()
        g2.first()
        for m in range(4):
            ga.fourth(m)
        ga.finish()
        unpack_small(r, n)
        near_bias(r)
        norm_first(r)
        project(r)

        def forward(p, c):
            attend_forward(r, p)

            @pl.when(p == 0)
            def _():
                for item in (g1, g2):
                    for m in (1, 2, 3):
                        item.second(m)

            @pl.when(p == 1)
            def _():
                for item in (g1, g2):
                    for m in range(4):
                        item.third(m)

            @pl.when(p == 2)
            def _():
                for item in (g1, g2):
                    for m in range(4):
                        item.fourth(m)

            return c

        lax.fori_loop(0, PAIRS, forward, 0)
        g1.finish()
        g2.finish()
        middle(r)

        def put_2(i, value):
            r.d2[i] = value.astype(bf16).reshape(8, r2, D)

        def put_1(i, value):
            r.d1[pl.ds(2 * i, 2)] = value.astype(bf16).reshape(2, 8, ra, ff)

        def put_o(i, value):
            r.dA[pl.ds(2 * i, 2), :, :, 3 * D : 4 * D] = value.astype(bf16).reshape(2, 8, ra, D)

        def put_a(i, value):
            r.dA[pl.ds(2 * i, 2), :, :, 0 : 3 * D] = value.astype(bf16).reshape(2, 8, ra, 3 * D)

        scatters = [
            Scatter(
                at,
                full,
                [s["buf%d_%d" % (i, j)] for j in range(6)],
                out,
                half,
                r.ssend.at[i],
                r.srecv.at[i],
            )
            for i, (full, out, (_, _, half)) in enumerate(
                zip((r.dA, r.d1, r.d2), (out_a, out_1, out_2), shapes)
            )
        ]
        sa, s1, s2 = scatters
        weight_grad(r.act, r.g, 512, put_2)
        s2.first()
        weight_grad(r.nf, r.gh, 256, put_1)
        s1.first()
        s2.second()
        weight_grad(r.att, r.gb, 256, put_o)

        def backward(p, c):
            attend_backward(r, p)

            @pl.when(p == 0)
            def _():
                s2.third()
                s1.second()

            @pl.when(p == 1)
            def _():
                s2.fourth()
                s1.third()

            @pl.when(p == 2)
            def _():
                s2.fifth()
                s1.fourth()

            return c

        lax.fori_loop(0, PAIRS, backward, 0)
        s1.fifth()
        table_grad(r)
        weight_grad(r.na, r.dproj, 256, put_a)
        last(r)
        tail = pack_small_grads(r, n).astype(bf16)
        r.dA[:, :, :, 4 * D :] = tail.reshape(4, 8, ra, 128)
        sa.first()
        sa.second()
        sa.third()
        sa.fourth()
        sa.fifth()
        for item in gathers + scatters:
            item.drain()

    out_shape = [
        jax.ShapeDtypeStruct((length, D), bf16),
        jax.ShapeDtypeStruct((length, D), f32),
        jax.ShapeDtypeStruct((ra, cols_a), f32),
        jax.ShapeDtypeStruct((ra, ff), f32),
        jax.ShapeDtypeStruct((r2, D), f32),
    ]
    operands = [x, documents, g, packed, w_a, w_o, w_1, w_2]
    return run_kernel(
        kernel, operands, out_shape, scratch, collective_id=0, has_side_effects=True
    )


def local_layer(x, documents, g, w_ao, w_1, w_2, sm, es, bd):
    length, ff = x.shape[0], w_1.shape[1]
    scratch = dict(work_scratch(length, ff))

    def kernel(ins, outs, s):
        r = types.SimpleNamespace(**s)
        r.x, r.docs, r.g, r.A, r.W1, r.W2, r.sm, r.es, r.bd = ins
        r.out, r.igrad, d_a, d_1, d_2, r.smg, r.esg, r.tg = outs
        masks(r)
        near_bias(r)
        norm_first(r)
        project(r)

        def forward(p, c):
            attend_forward(r, p)
            return c

        lax.fori_loop(0, PAIRS, forward, 0)
        middle(r)

        def put_into(ref, step, cols):
            def put(i, value):
                rows = pl.ds(pl.multiple_of(i * step, step), step)
                ref[rows, cols] = value.astype(ref.dtype)

            return put

        weight_grad(r.act, r.g, 512, put_into(d_2, 512, slice(None)))
        weight_grad(r.nf, r.gh, 256, put_into(d_1, 256, slice(None)))
        weight_grad(r.att, r.gb, 256, put_into(d_a, 256, slice(3 * D, 4 * D)))

        def backward(p, c):
            attend_backward(r, p)
            return c

        lax.fori_loop(0, PAIRS, backward, 0)
        table_grad(r)
        weight_grad(r.na, r.dproj, 256, put_into(d_a, 256, slice(0, 3 * D)))
        last(r)

    out_shape = [
        jax.ShapeDtypeStruct((length, D), bf16),
        jax.ShapeDtypeStruct((length, D), f32),
        jax.ShapeDtypeStruct((D, 4 * D), bf16),
        jax.ShapeDtypeStruct((D, ff), bf16),
        jax.ShapeDtypeStruct((ff, D), bf16),
        jax.ShapeDtypeStruct((16, D), f32),
        jax.ShapeDtypeStruct((8, ff), f32),
        jax.ShapeDtypeStruct((HEADS, 128), f32),
    ]
    return run_kernel(kernel, [x, documents, g, w_ao, w_1, w_2, sm, es, bd], out_shape, scratch)


def whole_body(dp_size, fsdp_size):
    def body(x, documents, fg, fs, w_a, table, w_o, os, sg, ss, w_1, es, w_2, rs, g):
        def row(v):
            return jnp.pad(v, (0, 128 - v.shape[0]))

        rows = [row(v) for v in (fg, fs, os, sg, ss, rs, es, table)]
        packed = jnp.concatenate([jnp.stack(rows), jnp.zeros((8, 128), bf16)], axis=0)
        out, igrad, d_a, d_1, d_2 = whole_layer(
            x, documents, g, packed, w_a, w_o, w_1, w_2, dp_size, fsdp_size
        )
        small = d_a[:, 4 * D :]

        def part(i, like):
            return small[i, : like.shape[0]]

        return (
            out,
            igrad,
            part(0, fg),
            part(1, fs),
            d_a[:, : 3 * D],
            part(7, table),
            d_a[:, 3 * D : 4 * D],
            part(2, os),
            part(3, sg),
            part(4, ss),
            d_1,
            part(6, es),
            d_2,
            part(5, rs),
        )

    return body


def split_body(x, documents, fg, fs, w_a, table, w_o, os, sg, ss, w_1, es, w_2, rs, g):
    def whole(v):
        return lax.all_gather(v, AXES, axis=0, tiled=True)

    def mine(v):
        return lax.psum_scatter(v.astype(f32), AXES, scatter_dimension=0, tiled=True)

    w_ao = whole(jnp.concatenate([w_a, w_o], axis=1))
    rows = [whole(v).astype(f32) for v in (fg, fs, os, sg, ss, rs)]
    sm = jnp.concatenate([jnp.stack(rows), jnp.zeros((10, D), f32)], axis=0)
    wide = whole(es).astype(f32)
    bias = whole(table).astype(f32).reshape(HEADS, BUCKETS)
    bd = bias[:, bucket_of(jnp.arange(256, dtype=jnp.int32))]
    out, igrad, d_a, d_1, d_2, smg, esg, tg = local_layer(
        x, documents, g, w_ao, whole(w_1), whole(w_2), sm, jnp.tile(wide[None], (8, 1)), bd
    )
    d_a = mine(d_a)
    return (
        out,
        igrad,
        mine(smg[0]),
        mine(smg[1]),
        d_a[:, : 3 * D],
        mine(tg[:, :BUCKETS].reshape(HEADS * BUCKETS)),
        d_a[:, 3 * D :],
        mine(smg[2]),
        mine(smg[3]),
        mine(smg[4]),
        mine(d_1),
        mine(esg[0]),
        mine(d_2),
        mine(smg[5]),
    )


def solution(mesh):
    rows, flat = P(AXES, None), P(AXES)
    dp_size, fsdp_size = mesh.shape["dp"], mesh.shape["fsdp"]
    one_kernel = (dp_size, fsdp_size) == (16, 2)
    return jax.shard_map(
        whole_body(dp_size, fsdp_size) if one_kernel else split_body,
        mesh=mesh,
        in_specs=(
            rows,
            rows,
            flat,
            flat,
            rows,
            flat,
            rows,
            flat,
            flat,
            flat,
            rows,
            flat,
            rows,
            flat,
            rows,
        ),
        out_specs=(rows, rows, flat, flat, rows, flat, rows, flat, flat, flat, rows, flat, rows, flat),
        check_vma=False,
    )
```

```python
import types

import jax
import jax.numpy as jnp
from jax import lax
from jax.experimental import pallas as pl
from jax.experimental.pallas import tpu as pltpu
from jax.sharding import PartitionSpec as P

D = 512
HEADS = 8
HEAD_DIM = 64
BUCKETS = 32
LONGEST = 512
TILE = 128
PAIRS = HEADS // 2
HALF = D // 2
BLOCK = 512
WIDE = 512
NEG = -1e30
eps = 1e-05
far_reach = 128

bf16 = jnp.bfloat16
f32 = jnp.float32
AXES = ("dp", "fsdp")


def iota(shape, dim):
    return lax.broadcasted_iota(jnp.int32, shape, dim)


def bucket_of(distance):
    exact_count = BUCKETS // 2
    counted = jnp.minimum(distance, exact_count)
    for level_j in range(1, exact_count):
        border = int(exact_count * (far_reach / exact_count) ** (level_j / exact_count))
        counted = counted + (distance >= border).astype(jnp.int32)
    return counted


def dot_nn(a, b):
    return lax.dot_general(a, b, (((1,), (0,)), ((), ())), preferred_element_type=f32)


def dot_nt(a, b):
    return lax.dot_general(a, b, (((1,), (1,)), ((), ())), preferred_element_type=f32)


def dot_tn(a, b):
    return lax.dot_general(a, b, (((0,), (0,)), ((), ())), preferred_element_type=f32)


def onehot(mask):
    return jnp.where(mask, 1.0, 0.0).astype(bf16)


def standardize(v):
    center = v - jnp.mean(v, axis=-1, keepdims=True)
    spread = jnp.mean(center * center, axis=-1, keepdims=True)
    rstd = lax.rsqrt(spread + eps)
    return center * rstd, rstd


def standardize_back(dx, xh, rstd):
    return rstd * (
        dx
        - jnp.mean(dx, axis=-1, keepdims=True)
        - xh * jnp.mean(dx * xh, axis=-1, keepdims=True)
    )


def gelu_parts(h):
    phi = 0.5 + 0.5 * lax.erf(h * 0.7071067811865476)
    return h * phi, phi + h * (0.3989422804014327 * jnp.exp(-0.5 * h * h))


def split_heads(t):
    top = iota(t.shape, 0) < HEAD_DIM
    zero = jnp.zeros_like(t)
    return jnp.concatenate([jnp.where(top, t, zero), jnp.where(top, zero, t)], axis=1)


def join_heads(t):
    n = t.shape[1] // 2
    return jnp.concatenate([t[:HEAD_DIM, :n], t[HEAD_DIM:, n:]], axis=0)


def unpack_small(r, n):
    packed = r.WH[0][:, 3 * HALF :]
    rows, lanes = iota((16 * n, D), 0), iota((16 * n, D), 1)
    per = D // n
    rep = onehot(iota((128, D), 1) % per == iota((128, D), 0))
    wide = dot_nn(packed, rep)
    wide = jnp.where(lanes // per == rows // 16, wide, 0.0)
    r.sm[...] = jnp.sum(wide.reshape(n, 16, D), axis=0)
    per = HEADS * BUCKETS // n
    group = BUCKETS // per
    pick = onehot(iota((n, 16 * n), 1) == 16 * iota((n, 16 * n), 0) + 7)
    bucket = bucket_of(iota((128, 256), 1))
    rep = onehot(bucket % per == iota((128, 256), 0))
    wide = dot_nn(dot_nn(pick, packed).astype(bf16), rep)
    bucket = bucket_of(iota((n, 256), 1))
    wide = jnp.where(bucket // per == iota((n, 256), 0) % group, wide, 0.0).astype(bf16)
    gather = onehot(iota((HEADS, n), 1) // group == iota((HEADS, n), 0))
    r.bd[...] = dot_nn(gather, wide)


def unpack_expand_shift(r, n):
    packed = r.WH[0][:, 3 * HALF :]
    ff = r.es.shape[1]
    per = ff // n
    pick = onehot(iota((n, 16 * n), 1) == 16 * iota((n, 16 * n), 0) + 6)
    rep = onehot(iota((128, ff), 1) % per == iota((128, ff), 0))
    wide = dot_nn(dot_nn(pick, packed).astype(bf16), rep)
    wide = jnp.where(iota((n, ff), 1) // per == iota((n, ff), 0), wide, 0.0)
    r.es[...] = jnp.broadcast_to(jnp.sum(wide, axis=0, keepdims=True), r.es.shape)


def pack_small_grads(r, n):
    rows, lanes = iota((16 * n, D), 0), iota((16 * n, D), 1)
    per = D // n
    wide = jnp.broadcast_to(r.smg[...][None], (n, 16, D)).reshape(16 * n, D)
    wide = jnp.where(lanes // per == rows // 16, wide, 0.0).astype(bf16)
    rep = onehot(iota((128, D), 1) % per == iota((128, D), 0))
    packed = dot_nt(wide, rep)
    ff = r.esg.shape[1]
    per = ff // n
    rep = onehot(iota((128, ff), 1) % per == iota((128, ff), 0))
    wide = jnp.broadcast_to(r.esg[0:1, :], (n, ff))
    wide = jnp.where(iota((n, ff), 1) // per == iota((n, ff), 0), wide, 0.0).astype(bf16)
    part = dot_nt(wide, rep).astype(bf16)
    place = onehot(iota((16 * n, n), 0) == 16 * iota((16 * n, n), 1) + 6)
    packed = packed + dot_nn(place, part)
    per = HEADS * BUCKETS // n
    group = BUCKETS // per
    spread = onehot(iota((n, HEADS), 0) // group == iota((n, HEADS), 1))
    wide = dot_nn(spread, r.tg[...].astype(bf16))
    wide = jnp.where(iota((n, 128), 1) // per == iota((n, 128), 0) % group, wide, 0.0)
    rep = onehot(iota((128, 128), 1) % per == iota((128, 128), 0))
    part = dot_nt(wide.astype(bf16), rep).astype(bf16)
    place = onehot(iota((16 * n, n), 0) == 16 * iota((16 * n, n), 1) + 7)
    return packed + dot_nn(place, part)


def over_rows(length, body, block=BLOCK, unroll=2):
    def rows(i, c):
        for u in range(unroll):
            body(pl.ds(pl.multiple_of((i * unroll + u) * block, block), block))
        return c

    lax.fori_loop(0, length // block // unroll, rows, 0)


def standardize_first(r):
    def rows(s):
        r.xh2[s, :] = standardize(r.x[s, :].astype(f32))[0]

    over_rows(r.x.shape[0], rows, 256, 1)


def norm_first(r):
    def rows(s):
        r.na[s, :] = (r.xh2[s, :] * r.sm[0:1, :] + r.sm[1:2, :]).astype(bf16)

    over_rows(r.x.shape[0], rows, 256, 1)


def masks(r):
    length = r.docs.shape[1]
    same = iota((128, length), 0) == r.docs[...]
    r.kd[...] = jnp.where(same, 1.0, 0.0).T.astype(bf16)
    differ = jnp.logical_and(iota((128, length), 0) < 8, jnp.logical_not(same))
    r.qd[...] = jnp.where(differ, NEG, 0.0).astype(bf16)


def near_bias(r):
    for h in range(HEADS):
        by_dist = r.bd[h : h + 1, :]
        by_dist = by_dist - by_dist[:, 255:256]
        line = jnp.concatenate([jnp.full((1, TILE), NEG, f32), by_dist], axis=1)
        line = jnp.broadcast_to(line, (TILE, 3 * TILE))
        line = pltpu.roll(line, 0, 1, stride=1, stride_axis=0)
        half = slice((h % 2) * TILE, (h % 2 + 1) * TILE)
        r.near[h // 2, 0:TILE, half] = line[:, 2 * TILE :]
        r.near[h // 2, TILE:, half] = line[:, TILE : 2 * TILE]


def project(r, half):
    def rows(s):
        out = dot_nn(r.na[s, :], r.WH[half][:, 0 : 3 * HALF])
        q = (out[:, :HALF].astype(bf16) * bf16(HEAD_DIM**-0.5)).T
        k = out[:, HALF : 2 * HALF].astype(bf16)
        v = out[:, 2 * HALF :].astype(bf16)
        for j in range(2):
            lanes = slice(j * 128, (j + 1) * 128)
            r.qt[2 * half + j, :, s] = q[lanes, :]
            r.k[2 * half + j, s, :] = k[:, lanes]
            r.v[2 * half + j, s, :] = v[:, lanes]

    over_rows(r.x.shape[0], rows)


def bands(length):
    first = 0
    for b in range(length // TILE):
        low = max(0, b - LONGEST // TILE)
        count = (b + 1 - low) * TILE
        yield b, slice(low * TILE, (b + 1) * TILE), slice(b * TILE, (b + 1) * TILE), first, count
        first += count


def band_rows(length):
    return sum(count for _, _, _, _, count in bands(length))


def attend_forward(r, p):
    near = r.near[p]
    lanes = pl.ds(pl.multiple_of(p * 128, 128), 128)
    plan = list(bands(r.x.shape[0]))

    def scores(b, ks, qs, first, count):
        qd = r.qd[:, qs]
        rhs = jnp.concatenate(
            [split_heads(r.qt[p, :, qs]), jnp.concatenate([qd, qd], axis=1)], axis=0
        )
        lhs = jnp.concatenate([r.k[p, ks, :], r.kd[ks, :]], axis=1)
        st = dot_nn(lhs, rhs)
        if count > 2 * TILE:
            return jnp.concatenate([st[: count - 2 * TILE], st[count - 2 * TILE :] + near], axis=0)
        return st + near[2 * TILE - count :]

    def soften(st, b, first, count):
        lifted = jnp.exp(st - jnp.max(st, axis=0, keepdims=True))
        inverse = 1.0 / jnp.sum(lifted, axis=0, keepdims=True)
        weights = lifted.astype(bf16)
        r.P[p, first : first + count, :] = weights
        r.inv[p, b : b + 1, :] = inverse
        return weights, inverse

    def attended(weights, inverse, ks, qs):
        ot = join_heads(dot_tn(r.v[p, ks, :], weights) * inverse)
        r.ot[p, :, qs] = ot
        r.att[qs, lanes] = ot.T.astype(bf16)

    AHEAD = 1
    queue, soft = [], []
    steps = len(plan)
    for i in range(steps + 2):
        if i < steps:
            queue.append(scores(*plan[i]))
        if 1 <= i <= steps:
            b, ks, qs, first, count = plan[i - 1]
            soft.append(soften(queue.pop(0), b, first, count))
        if 2 <= i:
            b, ks, qs, first, count = plan[i - 2]
            attended(*soft.pop(0), ks, qs)


def attend_backward(r, p):
    length = r.x.shape[0]
    r.dk[...] = jnp.zeros_like(r.dk)
    r.dv[...] = jnp.zeros_like(r.dv)
    r.acc[...] = jnp.zeros_like(r.acc)
    inner = pl.multiple_of((p // 2) * 3 * HALF + (p % 2) * 128, 128)
    top = iota((128, TILE), 0) < HEAD_DIM
    for b, ks, qs, first, count in bands(length):
        inverse = r.inv[p, b : b + 1, :]
        scale = jnp.where(top, inverse[:, :TILE], inverse[:, TILE:])
        dot_ = (r.dot[p, :, qs].astype(f32) * scale).astype(bf16)
        prod = dot_.astype(f32) * r.ot[p, :, qs]
        delta = jnp.concatenate(
            [
                jnp.sum(prod[:HEAD_DIM], axis=0, keepdims=True),
                jnp.sum(prod[HEAD_DIM:], axis=0, keepdims=True),
            ],
            axis=1,
        )
        dcat = split_heads(dot_)
        weights = r.P[p, first : first + count, :]
        ds = weights.astype(f32) * (dot_nn(r.v[p, ks, :], dcat) - delta)
        dsb = ds.astype(bf16)
        if count >= 2 * TILE:
            r.acc[...] += ds[count - 2 * TILE :]
        else:
            r.acc[TILE:, :] += ds
        r.dv[ks, :] += dot_nt(weights, dcat)
        r.dk[ks, :] += dot_nt(dsb, split_heads(r.qt[p, :, qs]))
        dqt = join_heads(dot_tn(r.k[p, ks, :], dsb)) * HEAD_DIM**-0.5
        r.act[qs, pl.ds(inner, 128)] = dqt.T.astype(bf16)
    r.act[:, pl.ds(HALF + inner, 128)] = r.dk[...].astype(bf16)
    r.act[:, pl.ds(2 * HALF + inner, 128)] = r.dv[...].astype(bf16)
    zero = jnp.zeros((TILE, TILE), f32)
    rows = iota((TILE, 3 * TILE), 0)
    for h in range(2):
        half = slice(h * TILE, (h + 1) * TILE)
        line = jnp.concatenate([zero, r.acc[TILE:, half], r.acc[:TILE, half]], axis=1)
        for bit in range(7):
            rolled = pltpu.roll(line, 3 * TILE - (1 << bit), 1)
            line = jnp.where((rows >> bit) & 1 == 1, rolled, line)
        r.lines[pl.ds(2 * p + h, 1), :] = jnp.sum(line, axis=0, keepdims=True)


def table_grad(r):
    by_dist = r.lines[:, TILE:]
    dist = iota((2 * TILE, 128), 0)
    near = jnp.logical_and(bucket_of(dist) == iota((2 * TILE, 128), 1), dist < 2 * TILE)
    near = jnp.logical_and(near, iota((2 * TILE, 128), 1) < BUCKETS - 1)
    counted = lax.dot_general(
        by_dist,
        jnp.where(near, 1.0, 0.0),
        (((1,), (0,)), ((), ())),
        precision=lax.Precision.HIGHEST,
        preferred_element_type=f32,
    )
    rest = -jnp.sum(counted, axis=1, keepdims=True)
    r.tg[...] = jnp.where(iota((HEADS, 128), 1) == BUCKETS - 1, rest, counted)


def before_ff(r):
    r.smg[...] = jnp.zeros_like(r.smg)
    r.esg[...] = jnp.zeros_like(r.esg)

    def rows(s):
        residual = r.x[s, :].astype(f32) + dot_nn(r.att[s, :], r.WO[...]) + r.sm[2:3, :]
        xh, rstd = standardize(residual)
        r.xh2[s, :] = xh
        r.rstd2[s, :] = rstd
        r.nf[s, :] = (xh * r.sm[3:4, :] + r.sm[4:5, :]).astype(bf16)
        r.branch[s, :] = residual + r.sm[5:6, :]

    over_rows(r.x.shape[0], rows)


def feed_forward(r, f):
    cols = slice(f * WIDE, (f + 1) * WIDE)
    half = r.W1[f // 2]
    inner = slice((f % 2) * WIDE, (f % 2 + 1) * WIDE)

    def rows(s):
        hidden = dot_nn(r.nf[s, :], half[:, inner]) + r.es[0:1, cols]
        active, slope = gelu_parts(hidden)
        r.act[s, cols] = active.astype(bf16)
        r.gh[s, cols] = slope.astype(bf16)

    over_rows(r.x.shape[0], rows, 256, 4)


def feed_backward(r, f):
    cols = slice(f * WIDE, (f + 1) * WIDE)

    def rows(s):
        gh = dot_nt(r.g[s, :], r.W2[cols, :]) * r.gh[s, cols].astype(f32)
        r.esg[0:1, cols] += jnp.sum(gh, axis=0, keepdims=True)
        r.gh[s, cols] = gh.astype(bf16)

    over_rows(r.x.shape[0], rows)


def after_ff(r, s):
    ff = r.es.shape[1]
    r.nf[s, :] = (r.branch[s, :] + dot_nn(r.act[s, :], r.W2[...])).astype(bf16)
    gnf = dot_nt(r.gh[s, : ff // 2], r.W1[0][...]) + dot_nt(r.gh[s, ff // 2 :], r.W1[1][...])
    xh = r.xh2[s, :]
    gf = r.g[s, :].astype(f32)
    grad = gf + standardize_back(gnf * r.sm[3:4, :], xh, r.rstd2[s, :])
    r.branch[s, :] = grad
    gb = grad.astype(bf16)
    r.gb[s, :] = gb
    r.smg[2:3, :] += jnp.sum(gb.astype(f32), axis=0, keepdims=True)
    r.smg[3:4, :] += jnp.sum(gnf * xh, axis=0, keepdims=True)
    r.smg[4:5, :] += jnp.sum(gnf, axis=0, keepdims=True)
    r.smg[5:6, :] += jnp.sum(gf, axis=0, keepdims=True)
    dot_ = dot_nt(gb, r.WO[...]).astype(bf16).T
    for p in range(PAIRS):
        r.dot[p, :, s] = dot_[p * 128 : (p + 1) * 128, :]


def half_columns(half):
    return slice(half * 3 * HALF, (half + 1) * 3 * HALF)


def pair_columns(ref, rows, p, base=0):
    at = base + (p % 2) * 128
    return jnp.concatenate(
        [ref[rows, part * HALF + at : part * HALF + at + 128] for part in range(3)], axis=1
    )


def back_project(r, half, pair=None):
    def rows(s):
        if pair is None:
            grads, weight = r.act[s, half_columns(half)], r.WH[half][:, 0 : 3 * HALF]
        else:
            grads = pair_columns(r.act, s, pair, half * 3 * HALF)
            weight = pair_columns(r.WH[half], slice(None), pair)
        part = dot_nt(grads, weight)
        r.gnf[s, :] = part if half == 0 else r.gnf[s, :] + part

    over_rows(r.x.shape[0], rows)


def last(r):
    def rows(s):
        gna = r.gnf[s, :]
        xh, rstd = standardize(r.x[s, :].astype(f32))
        r.xh2[s, :] = r.branch[s, :] + standardize_back(gna * r.sm[0:1, :], xh, rstd)
        r.smg[0:1, :] += jnp.sum(gna * xh, axis=0, keepdims=True)
        r.smg[1:2, :] += jnp.sum(gna, axis=0, keepdims=True)

    over_rows(r.x.shape[0], rows)


def weight_grad(left, right, step, put):
    count = left.shape[1] // step
    if count == 1:
        put(0, dot_tn(left[...], right()))
        return

    def rows(i, c):
        put(i, dot_tn(left[:, pl.ds(pl.multiple_of(i * step, step), step)], right()))
        return c

    lax.fori_loop(0, count, rows, 0)


class Place:
    def __init__(self, dp_size, fsdp_size):
        dp, x = lax.axis_index("dp"), lax.axis_index("fsdp")
        self.z, self.y, self.c, self.x = dp // 4, (dp // 2) % 2, dp % 2, x
        self.zs = dp_size // 4

    def zpeer(self, m):
        z = self.z
        return (z, z + 1 - 2 * (z % 2), (z + 2) % 4, 3 - z)[m]

    def index(self, m, t, other=False):
        x = 1 - self.x if t in (1, 3) else self.x
        y = 1 - self.y if t in (2, 3) else self.y
        c = 1 - self.c if other else self.c
        return ((self.zpeer(m) * 2 + y) * 2 + c) * 2 + x

    def inner(self, t, other=False):
        x = 1 - self.x if t in (1, 3) else self.x
        y = 1 - self.y if t in (2, 3) else self.y
        c = 1 - self.c if other else self.c
        return (y * 2 + c) * 2 + x

    def device(self, m=0, t=0, other=False):
        x = 1 - self.x if t in (1, 3) else self.x
        y = 1 - self.y if t in (2, 3) else self.y
        c = 1 - self.c if other else self.c
        return ((self.zpeer(m) * 2 + y) * 2 + c, x)

    def neighbours(self):
        return [self.device(m=m) for m in (1, 2, 3)] + [
            self.device(t=1),
            self.device(t=2),
            self.device(t=3),
            self.device(other=True),
        ]


def greet(place):
    barrier = pltpu.get_barrier_semaphore()
    for peer in place.neighbours():
        pl.semaphore_signal(
            barrier, inc=1, device_id=peer, device_id_type=pl.DeviceIdType.MESH
        )


def enter():
    pl.semaphore_wait(pltpu.get_barrier_semaphore(), 7)


GATHER_SEMS, SCATTER_SEMS = 35, 11
Z0, X0, Y0, OA0, OB0, S0 = -1, 3, 7, 11, 15, 19


class Gather:
    def __init__(self, place, whole, rho, half, send, recv):
        self.place, self.whole, self.rho, self.half = place, whole, rho, half
        self.send, self.recv = send, recv
        self.started = []

    def view(self, shard, part=None):
        rows = pl.ds(pl.multiple_of(shard * self.rho, 16), self.rho)
        if part is None:
            return self.whole.at[rows, :]
        cols = slice(0, self.half) if part == 0 else slice(self.half, self.whole.shape[1])
        return self.whole.at[rows, cols]

    def copy(self, shard, sem, device, part=None):
        ref = self.view(shard, part)
        return pltpu.make_async_remote_copy(
            src_ref=ref,
            dst_ref=ref,
            send_sem=self.send.at[sem],
            recv_sem=self.recv.at[sem],
            device_id=device,
            device_id_type=pl.DeviceIdType.MESH,
        )

    def start(self, shard, sem, device, part=None):
        self.copy(shard, sem, device, part).start()
        self.started.append((sem, part))

    def arrive(self, shard, sem, part=None):
        self.copy(shard, sem, self.place.device(other=True), part).wait_recv()

    def spread(self, m):
        at = self.place
        shard = at.index(m, 0)
        self.start(shard, X0 + m, at.device(t=1))
        self.start(shard, Y0 + m, at.device(t=2))
        if self.half is None:
            self.start(shard, OA0 + m, at.device(t=3))
        self.start(shard, S0 + m, at.device(other=True))

    def first(self):
        at = self.place
        for m in (1, 2, 3):
            self.start(at.index(0, 0), Z0 + m, at.device(m=m))
        self.spread(0)

    def second(self, m):
        self.arrive(self.place.index(m, 0), Z0 + m)
        self.spread(m)

    def third(self, m):
        at = self.place
        shard = at.index(m, 1)
        self.arrive(shard, X0 + m)
        if self.half is not None:
            self.start(shard, OA0 + m, at.device(t=2), 0)
        self.start(shard, S0 + 4 + m, at.device(other=True))
        shard = at.index(m, 2)
        self.arrive(shard, Y0 + m)
        if self.half is not None:
            self.start(shard, OB0 + m, at.device(t=1), 1)
        self.start(shard, S0 + 8 + m, at.device(other=True))

    def fourth(self, m):
        at = self.place
        shard = at.index(m, 3)
        if self.half is None:
            self.arrive(shard, OA0 + m)
        else:
            self.arrive(shard, OA0 + m, 0)
            self.arrive(shard, OB0 + m, 1)
        self.start(shard, S0 + 12 + m, at.device(other=True))

    def finish(self):
        for t in range(4):
            for m in range(4):
                self.arrive(self.place.index(m, t, other=True), S0 + 4 * t + m)

    def drain(self):
        at = self.place
        for sem, part in self.started:
            self.copy(at.index(0, 0), sem, at.device(other=True), part).wait_send()


class Scatter:
    def __init__(self, place, full, bufs, half, send, recv, emit):
        self.place, self.full, self.half, self.emit = place, full, half, emit
        self.sib, self.ra, self.rb, self.rx, self.ry, self.rz = bufs
        self.send, self.recv = send, recv
        self.started = []

    def copy(self, src, dst, sem, device):
        return pltpu.make_async_remote_copy(
            src_ref=src,
            dst_ref=dst,
            send_sem=self.send.at[sem],
            recv_sem=self.recv.at[sem],
            device_id=device,
            device_id_type=pl.DeviceIdType.MESH,
        )

    def start(self, src, dst, sem, device):
        self.copy(src, dst, sem, device).start()
        self.started.append(sem)

    def arrive(self, dst, sem):
        self.copy(dst, dst, sem, self.place.device(other=True)).wait_recv()

    def first(self):
        at = self.place
        for t in (3, 1, 2, 0):
            self.start(
                self.full.at[:, at.inner(t, other=True)], self.sib.at[t], t, at.device(other=True)
            )

    def merge(self, t):
        self.arrive(self.sib.at[t], t)
        self.sib[t] += self.full[:, self.place.inner(t)]

    def second(self):
        at = self.place
        self.merge(3)
        if self.half is None:
            self.start(self.sib.at[3], self.ra, 4, at.device(t=3))
            self.merge(1)
            self.start(self.sib.at[1], self.rx, 6, at.device(t=1))
            self.merge(2)
            self.start(self.sib.at[2], self.ry, 7, at.device(t=2))
        else:
            self.start(self.sib.at[3, :, :, : self.half], self.ra, 4, at.device(t=1))
            self.start(self.sib.at[3, :, :, self.half :], self.rb, 5, at.device(t=2))

    def third(self):
        at = self.place
        if self.half is None:
            return
        self.merge(1)
        self.merge(2)
        self.arrive(self.rb, 5)
        self.sib[1, :, :, self.half :] += self.rb[...]
        self.start(self.sib.at[1], self.rx, 6, at.device(t=1))
        self.arrive(self.ra, 4)
        self.sib[2, :, :, : self.half] += self.ra[...]
        self.start(self.sib.at[2], self.ry, 7, at.device(t=2))

    def fourth(self):
        at = self.place
        self.merge(0)
        self.arrive(self.rx, 6)
        self.arrive(self.ry, 7)
        total = self.rx[...].astype(f32) + self.ry[...].astype(f32)
        if self.half is None:
            self.arrive(self.ra, 4)
            total = total + self.ra[...].astype(f32)
        self.sib[0] += total.astype(bf16)
        for m in (1, 2, 3):
            self.start(self.sib.at[0, at.zpeer(m)], self.rz.at[m - 1], 7 + m, at.device(m=m))

    def fifth(self):
        total = self.sib[0, self.place.z].astype(f32)
        for m in (1, 2, 3):
            self.arrive(self.rz.at[m - 1], 7 + m)
            total = total + self.rz[m - 1].astype(f32)
        self.emit(total)

    def drain(self):
        for sem in self.started:
            if sem < 4:
                dst = self.sib.at[sem]
            elif sem < 8:
                dst = (self.ra, self.rb, self.rx, self.ry)[sem - 4]
            else:
                dst = self.rz.at[sem - 8]
            self.copy(dst, dst, sem, self.place.device(other=True)).wait_send()


def scatter_bufs(rho, cols, half):
    first = cols if half is None else half
    rest = 128 if half is None else cols - half
    return [
        pltpu.VMEM((4, 4, rho, cols), bf16),
        pltpu.VMEM((4, rho, first), bf16),
        pltpu.VMEM((4, rho, rest), bf16),
        pltpu.VMEM((4, rho, cols), bf16),
        pltpu.VMEM((4, rho, cols), bf16),
        pltpu.VMEM((3, rho, cols), bf16),
    ]


def over_pairs(attend, r, first, end, pump):
    def one(p, c):
        attend(r, p)
        for pair in range(first, end):
            if pair in pump:

                @pl.when(p == pair)
                def _():
                    pump[pair]()
        return c

    lax.fori_loop(first, end, one, 0)


def work_scratch(length, ff):
    tokens = band_rows(length)
    return dict(
        x=pltpu.VMEM((length, D), bf16),
        na=pltpu.VMEM((length, D), bf16),
        kd=pltpu.VMEM((length, 128), bf16),
        qd=pltpu.VMEM((128, length), bf16),
        near=pltpu.VMEM((PAIRS, 2 * TILE, 2 * TILE), f32),
        qt=pltpu.VMEM((PAIRS, 128, length), bf16),
        k=pltpu.VMEM((PAIRS, length, 128), bf16),
        v=pltpu.VMEM((PAIRS, length, 128), bf16),
        P=pltpu.VMEM((PAIRS, tokens, 2 * TILE), bf16),
        inv=pltpu.VMEM((PAIRS, length // TILE, 2 * TILE), f32),
        ot=pltpu.VMEM((PAIRS, 128, length), f32),
        att=pltpu.VMEM((length, D), bf16),
        xh2=pltpu.VMEM((length, D), f32),
        rstd2=pltpu.VMEM((length, 1), f32),
        branch=pltpu.VMEM((length, D), f32),
        gnf=pltpu.VMEM((length, D), f32),
        nf=pltpu.VMEM((length, D), bf16),
        act=pltpu.VMEM((length, ff), bf16),
        gh=pltpu.VMEM((length, ff), bf16),
        gb=pltpu.VMEM((length, D), bf16),
        dot=pltpu.VMEM((PAIRS, 128, length), bf16),
        dk=pltpu.VMEM((length, 128), f32),
        dv=pltpu.VMEM((length, 128), f32),
        acc=pltpu.VMEM((2 * TILE, 2 * TILE), f32),
        lines=pltpu.VMEM((HEADS, 3 * TILE), f32),
    )


def small_scratch(ff):
    return dict(
        sm=pltpu.VMEM((16, D), f32),
        es=pltpu.VMEM((8, ff), f32),
        bd=pltpu.VMEM((HEADS, 256), f32),
        smg=pltpu.VMEM((16, D), f32),
        esg=pltpu.VMEM((8, ff), f32),
        tg=pltpu.VMEM((HEADS, 128), f32),
    )


def run_kernel(kernel, operands, out_shape, scratch, in_hbm=(), out_hbm=(), **params):
    names = list(scratch)
    count = len(operands) + len(out_shape)

    def named(*refs):
        kernel(refs[: len(operands)], refs[len(operands) : count], dict(zip(names, refs[count:])))

    def specs(number, hbm):
        return [
            pl.BlockSpec(memory_space=pl.ANY if i in hbm else pltpu.VMEM) for i in range(number)
        ]

    return pl.pallas_call(
        named,
        out_shape=out_shape,
        in_specs=specs(len(operands), in_hbm),
        out_specs=specs(len(out_shape), out_hbm),
        scratch_shapes=[scratch[name] for name in names],
        compiler_params=pltpu.CompilerParams(vmem_limit_bytes=VMEM_BYTES, **params),
    )(*operands)


VMEM_BYTES = 63 * 1024 * 1024


def whole_layer(x, documents, g, small, w_a, w_o, w_1, w_2, dp_size, fsdp_size):
    n = dp_size * fsdp_size
    length, ff = x.shape[0], w_1.shape[1]
    ra, r2 = w_1.shape[0], w_2.shape[0]
    gathered = dict(
        H0=(ra, 3 * HALF + 128, None),
        H1=(ra, 3 * HALF, None),
        WO=(ra, D, HALF),
        W2=(r2, D, HALF),
        W1a=(ra, ff // 2, ff // 4),
        W1b=(ra, ff // 2, ff // 4),
    )
    scattered = dict(
        d1a=(ra, ff // 2, ff // 4),
        d1b=(ra, ff // 2, ff // 4),
        d2a=(r2, D // 2, 128),
        d2b=(r2, D // 2, 128),
        dO=(ra, D, HALF),
        dH=(ra, 3 * HALF, HALF),
        dT2=(ra, 384, 128),
        dT3=(ra, 384, None),
        dS=(ra, 128, None),
    )
    scratch = dict(work_scratch(length, ff), **small_scratch(ff))
    scratch["g"] = pltpu.VMEM((length, D), bf16)
    for name, (rho, cols, _) in gathered.items():
        scratch[name] = pltpu.VMEM((n * rho, cols), bf16)
    for name, (rho, cols, half) in scattered.items():
        scratch[name] = pltpu.VMEM((4, 8, rho, cols), bf16)
        for j, buf in enumerate(scatter_bufs(rho, cols, half)):
            scratch["%s_%d" % (name, j)] = buf
    dma = pltpu.SemaphoreType.DMA
    scratch.update(
        gsend=dma((len(gathered), GATHER_SEMS)),
        grecv=dma((len(gathered), GATHER_SEMS)),
        ssend=dma((len(scattered), SCATTER_SEMS)),
        srecv=dma((len(scattered), SCATTER_SEMS)),
        move=dma((4,)),
    )

    def kernel(ins, outs, s):
        r = types.SimpleNamespace(**s)
        x_in, r.docs, g_in = ins[:3]
        vectors, (own_a, own_o, own_1, own_2) = ins[3:11], ins[11:]
        out, igrad, out_a, out_o, out_1, out_2, out_s = outs
        r.WH, r.W1 = [r.H0, r.H1], [r.W1a, r.W1b]
        at = Place(dp_size, fsdp_size)
        get_x = pltpu.make_async_copy(x_in, r.x, r.move.at[0])
        get_g = pltpu.make_async_copy(g_in, r.g, r.move.at[1])
        put_out = pltpu.make_async_copy(r.nf, out, r.move.at[2])
        put_igrad = pltpu.make_async_copy(r.xh2, igrad, r.move.at[3])
        get_x.start()
        get_g.start()
        greet(at)
        mine = at.index(0, 0)
        rows_a = pl.ds(pl.multiple_of(mine * ra, 16), ra)
        rows_2 = pl.ds(pl.multiple_of(mine * r2, 16), r2)
        for half, ref in enumerate(r.WH):
            for part in range(3):
                ref[rows_a, part * HALF : (part + 1) * HALF] = own_a[
                    :, part * D + half * HALF : part * D + (half + 1) * HALF
                ]
        lines = [
            jnp.concatenate(
                [v[...].astype(f32), jnp.zeros((1, 128 - v.shape[1]), f32)], axis=1
            )
            for v in vectors
        ]
        lines.append(jnp.zeros((ra - len(lines), 128), f32))
        r.H0[rows_a, 3 * HALF :] = jnp.concatenate(lines, axis=0).astype(bf16)
        r.WO[rows_a, :] = own_o[...]
        r.W2[rows_2, :] = own_2[...]
        for half, ref in enumerate(r.W1):
            ref[rows_a, :] = own_1[:, half * ff // 2 : (half + 1) * ff // 2]
        gathers = {
            name: Gather(at, s[name], rho, half, r.gsend.at[i], r.grecv.at[i])
            for i, (name, (rho, _, half)) in enumerate(gathered.items())
        }
        h0, h1, wo, w2, w1a, w1b = gathers.values()
        every = (0, 1, 2, 3)

        def seconds(item):
            for m in every[1:]:
                item.second(m)

        def thirds(item):
            for m in every:
                item.third(m)

        def fourths(item):
            for m in every:
                item.fourth(m)

        enter()
        h0.first()
        masks(r)
        get_x.wait()
        standardize_first(r)
        seconds(h0)
        h1.first()
        wo.first()
        thirds(h0)
        fourths(h0)
        seconds(h1)
        w1a.first()
        seconds(wo)
        h0.finish()
        unpack_small(r, n)
        norm_first(r)
        near_bias(r)
        project(r, 0)
        w1b.first()
        thirds(h1)
        fourths(h1)
        seconds(w1a)
        pump = {
            0: lambda: (thirds(wo), w2.first()),
            1: lambda: (thirds(w1a), seconds(w1b), h1.finish()),
            2: lambda: (fourths(wo), seconds(w2)),
            3: lambda: (fourths(w1a), thirds(w1b), wo.finish()),
        }
        over_pairs(attend_forward, r, 0, 2, pump)
        project(r, 1)
        over_pairs(attend_forward, r, 2, 4, pump)
        unpack_expand_shift(r, n)
        before_ff(r)
        w1a.finish()
        feed_forward(r, 0)
        fourths(w1b)
        feed_forward(r, 1)
        thirds(w2)
        w1b.finish()
        feed_forward(r, 2)
        feed_forward(r, 3)
        fourths(w2)
        get_g.wait()

        def emit_into(ref, cols):
            def emit(total):
                ref[:, cols] = total

            return emit

        def emit_pairs(pairs):
            def emit(total):
                wide = 128 * len(pairs)
                for part in range(3):
                    first = part * D + pairs[0] * 128
                    out_a[:, first : first + wide] = total[:, part * wide : (part + 1) * wide]

            return emit

        emits = dict(
            d1a=emit_into(out_1, slice(0, ff // 2)),
            d1b=emit_into(out_1, slice(ff // 2, ff)),
            d2a=emit_into(out_2, slice(0, D // 2)),
            d2b=emit_into(out_2, slice(D // 2, D)),
            dO=emit_into(out_o, slice(None)),
            dH=emit_pairs((0, 1)),
            dT2=emit_pairs((2,)),
            dT3=emit_pairs((3,)),
            dS=emit_into(out_s, slice(None)),
        )
        scatters = {
            name: Scatter(
                at,
                s[name],
                [s["%s_%d" % (name, j)] for j in range(6)],
                half,
                r.ssend.at[i],
                r.srecv.at[i],
                emits[name],
            )
            for i, (name, (_, _, half)) in enumerate(scattered.items())
        }
        s1a, s1b, s2a, s2b, so, sh, st2, st3, ss = scatters.values()

        def put_shards(ref, step, rho, first=0):
            count = step // (8 * rho)

            def put(i, value):
                value = value.astype(bf16).reshape(count, 8, rho, value.shape[1])
                ref[pl.ds(count * i, count), :, :, first : first + value.shape[3]] = value

            return put

        def put_two(i, value):
            value = value.astype(bf16).reshape(2, 8, r2, D)
            r.d2a[pl.ds(2 * i, 2)] = value[:, :, :, : D // 2]
            r.d2b[pl.ds(2 * i, 2)] = value[:, :, :, D // 2 :]

        def expand_grad(f, ref):
            cols = slice(f * WIDE, (f + 1) * WIDE)
            weight_grad(
                r.nf, lambda: r.gh[:, cols], D, put_shards(ref, D, ra, (f % 2) * WIDE)
            )

        weight_grad(r.act, lambda: r.g[...], 1024, put_two)
        s2a.first()
        s2b.first()
        w2.finish()
        feed_backward(r, 0)
        expand_grad(0, r.d1a)
        feed_backward(r, 1)
        expand_grad(1, r.d1a)
        s2a.second()
        s1a.first()
        feed_backward(r, 2)
        expand_grad(2, r.d1b)
        feed_backward(r, 3)
        expand_grad(3, r.d1b)
        s2b.second()
        s1b.first()
        after_ff(r, slice(0, BLOCK))
        s1a.second()
        s2a.third()
        for i in range(1, length // BLOCK):
            after_ff(r, slice(i * BLOCK, (i + 1) * BLOCK))
        put_out.start()
        s1b.second()
        s2b.third()
        weight_grad(r.att, lambda: r.gb[...], D, put_shards(r.dO, D, ra))
        so.first()
        pump = {
            0: lambda: (so.second(), s1a.third(), s2a.fourth()),
            1: lambda: (s1b.third(), s2b.fourth()),
            2: lambda: (sh.second(), so.third(), s1a.fourth(), s2a.fifth()),
            3: lambda: (st2.second(), sh.third(), so.fourth(), s1b.fourth(), s2b.fifth()),
        }
        over_pairs(attend_backward, r, 0, 2, pump)
        weight_grad(
            r.na, lambda: r.act[:, half_columns(0)], D, put_shards(r.dH, D, ra)
        )
        sh.first()
        back_project(r, 0)
        over_pairs(attend_backward, r, 2, 3, pump)
        weight_grad(
            r.na, lambda: pair_columns(r.act, slice(None), 2, 3 * HALF), D, put_shards(r.dT2, D, ra)
        )
        st2.first()
        back_project(r, 1, 2)
        over_pairs(attend_backward, r, 3, 4, pump)
        weight_grad(
            r.na, lambda: pair_columns(r.act, slice(None), 3, 3 * HALF), D, put_shards(r.dT3, D, ra)
        )
        st3.first()
        back_project(r, 1, 3)
        last(r)
        put_igrad.start()
        st3.second()
        table_grad(r)
        r.dS[...] = pack_small_grads(r, n).astype(bf16).reshape(4, 8, ra, 128)
        ss.first()
        sh.fourth()
        st2.third()
        s1a.fifth()
        ss.second()
        so.fifth()
        s1b.fifth()
        st2.fourth()
        st3.fourth()
        ss.fourth()
        sh.fifth()
        st2.fifth()
        st3.fifth()
        ss.fifth()
        for item in list(gathers.values()) + list(scatters.values()):
            item.drain()
        put_out.wait()
        put_igrad.wait()

    out_shape = [
        jax.ShapeDtypeStruct((length, D), bf16),
        jax.ShapeDtypeStruct((length, D), f32),
        jax.ShapeDtypeStruct((ra, 3 * D), f32),
        jax.ShapeDtypeStruct((ra, D), f32),
        jax.ShapeDtypeStruct((ra, ff), f32),
        jax.ShapeDtypeStruct((r2, D), f32),
        jax.ShapeDtypeStruct((ra, 128), f32),
    ]
    operands = [x, documents, g, *small, w_a, w_o, w_1, w_2]
    return run_kernel(
        kernel,
        operands,
        out_shape,
        scratch,
        in_hbm=(0, 2),
        out_hbm=(0, 1),
        collective_id=0,
        has_side_effects=True,
    )


def hand_out(results, sizes):
    length = results[0].shape[0]
    chunk = length // 2

    def kernel(ins, outs, s):
        buffers = (s["a"], s["b"])

        def move(i, j, back):
            rows = slice(j * chunk, (j + 1) * chunk)
            here = buffers[i].at[rows, :]
            there = (outs if back else ins)[i].at[rows, :]
            sem = s["move"].at[2 * i + j, int(back)]
            if back:
                return pltpu.make_async_copy(here, there, sem)
            return pltpu.make_async_copy(there, here, sem)

        parts = [(i, j) for j in range(2) for i in range(2)]
        for i, j in parts:
            move(i, j, False).start()
        for i in range(2, 6):
            outs[i][...] = ins[i][...]
        for i, size in enumerate(sizes):
            outs[6 + i][...] = ins[6][i : i + 1, :size]
        for i, j in parts:
            move(i, j, False).wait()
            move(i, j, True).start()
        for i, j in parts:
            move(i, j, True).wait()

    out_shape = [jax.ShapeDtypeStruct(v.shape, v.dtype) for v in results[:6]]
    out_shape += [jax.ShapeDtypeStruct((1, size), f32) for size in sizes]
    scratch = dict(
        a=pltpu.VMEM(results[0].shape, results[0].dtype),
        b=pltpu.VMEM(results[1].shape, results[1].dtype),
        move=pltpu.SemaphoreType.DMA((4, 2)),
    )
    return run_kernel(
        kernel, list(results), out_shape, scratch, in_hbm=(0, 1), out_hbm=(0, 1)
    )


def local_layer(x, documents, g, h0, h1, w_o, w_1a, w_1b, w_2, sm, es, bd):
    length, ff = x.shape[0], 2 * w_1a.shape[1]
    scratch = dict(work_scratch(length, ff))

    def kernel(ins, outs, s):
        r = types.SimpleNamespace(**s)
        x_in, r.docs, r.g, h0_, h1_, r.WO, w1a_, w1b_, r.W2, r.sm, r.es, r.bd = ins
        out, igrad, d_a, d_o, d_1, d_2, r.smg, r.esg, r.tg = outs
        r.WH, r.W1 = [h0_, h1_], [w1a_, w1b_]
        r.x[...] = x_in[...]
        masks(r)
        near_bias(r)
        standardize_first(r)
        norm_first(r)
        project(r, 0)
        project(r, 1)

        over_pairs(attend_forward, r, 0, PAIRS, {})
        before_ff(r)

        def put_into(ref, step, first, wide):
            def put(i, value):
                rows = pl.ds(pl.multiple_of(i * step, step), step)
                ref[rows, first : first + wide] = value.astype(ref.dtype)

            return put

        for f in range(ff // WIDE):
            feed_forward(r, f)
        weight_grad(r.act, lambda: r.g[...], 1024, put_into(d_2, 1024, 0, D))
        for f in range(ff // WIDE):
            cols = slice(f * WIDE, (f + 1) * WIDE)
            feed_backward(r, f)
            weight_grad(
                r.nf, lambda cols=cols: r.gh[:, cols], D, put_into(d_1, D, f * WIDE, WIDE)
            )
        for i in range(length // BLOCK):
            after_ff(r, slice(i * BLOCK, (i + 1) * BLOCK))
        out[...] = r.nf[...]
        weight_grad(r.att, lambda: r.gb[...], D, put_into(d_o, D, 0, D))
        over_pairs(attend_backward, r, 0, PAIRS, {})
        for half in range(2):
            back_project(r, half)

            def put(i, value, half=half):
                for part in range(3):
                    first = part * D + half * HALF
                    d_a[:, first : first + HALF] = value[
                        :, part * HALF : (part + 1) * HALF
                    ].astype(bf16)

            weight_grad(r.na, lambda half=half: r.act[:, half_columns(half)], D, put)
        last(r)
        table_grad(r)
        igrad[...] = r.xh2[...]

    out_shape = [
        jax.ShapeDtypeStruct((length, D), bf16),
        jax.ShapeDtypeStruct((length, D), f32),
        jax.ShapeDtypeStruct((D, 3 * D), bf16),
        jax.ShapeDtypeStruct((D, D), bf16),
        jax.ShapeDtypeStruct((D, ff), bf16),
        jax.ShapeDtypeStruct((ff, D), bf16),
        jax.ShapeDtypeStruct((16, D), f32),
        jax.ShapeDtypeStruct((8, ff), f32),
        jax.ShapeDtypeStruct((HEADS, 128), f32),
    ]
    operands = [x, documents, g, h0, h1, w_o, w_1a, w_1b, w_2, sm, es, bd]
    return run_kernel(kernel, operands, out_shape, scratch)


def whole_body(dp_size, fsdp_size):
    def body(x, documents, fg, fs, w_a, table, w_o, os, sg, ss, w_1, es, w_2, rs, g):
        vectors = (fg, fs, os, sg, ss, rs, es, table)
        results = whole_layer(
            x,
            documents,
            g,
            [v.reshape(1, -1) for v in vectors],
            w_a,
            w_o,
            w_1,
            w_2,
            dp_size,
            fsdp_size,
        )
        out, igrad, d_a, d_o, d_1, d_2, *small = hand_out(
            results, [v.shape[0] for v in vectors]
        )
        dfg, dfs, dos, dsg, dss, drs, des, dtable = [v.reshape(-1) for v in small]
        return (out, igrad, dfg, dfs, d_a, dtable, d_o, dos, dsg, dss, d_1, des, d_2, drs)

    return body


def split_body(x, documents, fg, fs, w_a, table, w_o, os, sg, ss, w_1, es, w_2, rs, g):
    def whole(v):
        return lax.all_gather(v, AXES, axis=0, tiled=True)

    def mine(v):
        return lax.psum_scatter(v.astype(f32), AXES, scatter_dimension=0, tiled=True)

    parts = [w_a[:, i * HALF : (i + 1) * HALF] for i in range(6)]
    h0 = whole(jnp.concatenate(parts[0::2], axis=1))
    h1 = whole(jnp.concatenate(parts[1::2], axis=1))
    ff = w_1.shape[1]
    rows = [whole(v).astype(f32) for v in (fg, fs, os, sg, ss, rs)]
    sm = jnp.concatenate([jnp.stack(rows), jnp.zeros((10, D), f32)], axis=0)
    wide = jnp.tile(whole(es).astype(f32)[None], (8, 1))
    bias = whole(table).astype(f32).reshape(HEADS, BUCKETS)
    bd = bias[:, bucket_of(jnp.arange(256, dtype=jnp.int32))]
    w_1 = whole(w_1)
    out, igrad, d_a, d_o, d_1, d_2, smg, esg, tg = local_layer(
        x,
        documents,
        g,
        h0,
        h1,
        whole(w_o),
        w_1[:, : ff // 2],
        w_1[:, ff // 2 :],
        whole(w_2),
        sm,
        wide,
        bd,
    )
    return (
        out,
        igrad,
        mine(smg[0]),
        mine(smg[1]),
        mine(d_a),
        mine(tg[:, :BUCKETS].reshape(HEADS * BUCKETS)),
        mine(d_o),
        mine(smg[2]),
        mine(smg[3]),
        mine(smg[4]),
        mine(d_1),
        mine(esg[0]),
        mine(d_2),
        mine(smg[5]),
    )


def solution(mesh):
    rows, flat = P(AXES, None), P(AXES)
    dp_size, fsdp_size = mesh.shape["dp"], mesh.shape["fsdp"]
    one_kernel = (dp_size, fsdp_size) == (16, 2)
    return jax.shard_map(
        whole_body(dp_size, fsdp_size) if one_kernel else split_body,
        mesh=mesh,
        in_specs=(
            rows,
            rows,
            flat,
            flat,
            rows,
            flat,
            rows,
            flat,
            flat,
            flat,
            rows,
            flat,
            rows,
            flat,
            rows,
        ),
        out_specs=(rows, rows, flat, flat, rows, flat, rows, flat, flat, flat, rows, flat, rows, flat),
        check_vma=False,
    )
```

```python
import types

import jax
import jax.numpy as jnp
from jax import lax
from jax.experimental import pallas as pl
from jax.experimental.pallas import tpu as pltpu
from jax.sharding import PartitionSpec as P

D = 512
HEADS = 8
HEAD_DIM = 64
BUCKETS = 32
LONGEST = 512
TILE = 128
PAIRS = HEADS // 2
HALF = D // 2
BLOCK = 512
WIDE = 512
NEG = -1e30
eps = 1e-05
far_reach = 128

bf16 = jnp.bfloat16
f32 = jnp.float32
AXES = ("dp", "fsdp")


def iota(shape, dim):
    return lax.broadcasted_iota(jnp.int32, shape, dim)


def bucket_of(distance):
    exact_count = BUCKETS // 2
    counted = jnp.minimum(distance, exact_count)
    for level_j in range(1, exact_count):
        border = int(exact_count * (far_reach / exact_count) ** (level_j / exact_count))
        counted = counted + (distance >= border).astype(jnp.int32)
    return counted


def dot_nn(a, b):
    return lax.dot_general(a, b, (((1,), (0,)), ((), ())), preferred_element_type=f32)


def dot_nt(a, b):
    return lax.dot_general(a, b, (((1,), (1,)), ((), ())), preferred_element_type=f32)


def dot_tn(a, b):
    return lax.dot_general(a, b, (((0,), (0,)), ((), ())), preferred_element_type=f32)


def onehot(mask):
    return jnp.where(mask, 1.0, 0.0).astype(bf16)


def standardize(v):
    center = v - jnp.mean(v, axis=-1, keepdims=True)
    spread = jnp.mean(center * center, axis=-1, keepdims=True)
    rstd = lax.rsqrt(spread + eps)
    return center * rstd, rstd


def standardize_back(dx, xh, rstd):
    return rstd * (
        dx
        - jnp.mean(dx, axis=-1, keepdims=True)
        - xh * jnp.mean(dx * xh, axis=-1, keepdims=True)
    )


def gelu_parts(h):
    phi = 0.5 + 0.5 * lax.erf(h * 0.7071067811865476)
    return h * phi, phi + h * (0.3989422804014327 * jnp.exp(-0.5 * h * h))


def split_heads(t):
    top = iota(t.shape, 0) < HEAD_DIM
    zero = jnp.zeros_like(t)
    return jnp.concatenate([jnp.where(top, t, zero), jnp.where(top, zero, t)], axis=1)


def join_heads(t):
    n = t.shape[1] // 2
    return jnp.concatenate([t[:HEAD_DIM, :n], t[HEAD_DIM:, n:]], axis=0)


def unpack_small(r, n):
    packed = r.WH[0][:, 3 * HALF :]
    rows, lanes = iota((16 * n, D), 0), iota((16 * n, D), 1)
    per = D // n
    rep = onehot(iota((128, D), 1) % per == iota((128, D), 0))
    wide = dot_nn(packed, rep)
    wide = jnp.where(lanes // per == rows // 16, wide, 0.0)
    r.sm[...] = jnp.sum(wide.reshape(n, 16, D), axis=0)
    per = HEADS * BUCKETS // n
    group = BUCKETS // per
    pick = onehot(iota((n, 16 * n), 1) == 16 * iota((n, 16 * n), 0) + 7)
    bucket = bucket_of(iota((128, 256), 1))
    rep = onehot(bucket % per == iota((128, 256), 0))
    wide = dot_nn(dot_nn(pick, packed).astype(bf16), rep)
    bucket = bucket_of(iota((n, 256), 1))
    wide = jnp.where(bucket // per == iota((n, 256), 0) % group, wide, 0.0).astype(bf16)
    gather = onehot(iota((HEADS, n), 1) // group == iota((HEADS, n), 0))
    r.bd[...] = dot_nn(gather, wide)


def unpack_expand_shift(r, n):
    packed = r.WH[0][:, 3 * HALF :]
    ff = r.es.shape[1]
    per = ff // n
    pick = onehot(iota((n, 16 * n), 1) == 16 * iota((n, 16 * n), 0) + 6)
    rep = onehot(iota((128, ff), 1) % per == iota((128, ff), 0))
    wide = dot_nn(dot_nn(pick, packed).astype(bf16), rep)
    wide = jnp.where(iota((n, ff), 1) // per == iota((n, ff), 0), wide, 0.0)
    r.es[...] = jnp.broadcast_to(jnp.sum(wide, axis=0, keepdims=True), r.es.shape)


def pack_small_grads(r, n):
    rows, lanes = iota((16 * n, D), 0), iota((16 * n, D), 1)
    per = D // n
    wide = jnp.broadcast_to(r.smg[...][None], (n, 16, D)).reshape(16 * n, D)
    wide = jnp.where(lanes // per == rows // 16, wide, 0.0).astype(bf16)
    rep = onehot(iota((128, D), 1) % per == iota((128, D), 0))
    packed = dot_nt(wide, rep)
    ff = r.esg.shape[1]
    per = ff // n
    rep = onehot(iota((128, ff), 1) % per == iota((128, ff), 0))
    wide = jnp.broadcast_to(r.esg[0:1, :], (n, ff))
    wide = jnp.where(iota((n, ff), 1) // per == iota((n, ff), 0), wide, 0.0).astype(bf16)
    part = dot_nt(wide, rep).astype(bf16)
    place = onehot(iota((16 * n, n), 0) == 16 * iota((16 * n, n), 1) + 6)
    packed = packed + dot_nn(place, part)
    per = HEADS * BUCKETS // n
    group = BUCKETS // per
    spread = onehot(iota((n, HEADS), 0) // group == iota((n, HEADS), 1))
    wide = dot_nn(spread, r.tg[...].astype(bf16))
    wide = jnp.where(iota((n, 128), 1) // per == iota((n, 128), 0) % group, wide, 0.0)
    rep = onehot(iota((128, 128), 1) % per == iota((128, 128), 0))
    part = dot_nt(wide.astype(bf16), rep).astype(bf16)
    place = onehot(iota((16 * n, n), 0) == 16 * iota((16 * n, n), 1) + 7)
    return packed + dot_nn(place, part)


def over_rows(length, body, block=BLOCK, unroll=2):
    def rows(i, c):
        for u in range(unroll):
            body(pl.ds(pl.multiple_of((i * unroll + u) * block, block), block))
        return c

    lax.fori_loop(0, length // block // unroll, rows, 0)


def standardize_first(r):
    def rows(s):
        r.xh2[s, :] = standardize(r.x[s, :].astype(f32))[0]

    over_rows(r.x.shape[0], rows, 256, 1)


def norm_first(r):
    def rows(s):
        r.na[s, :] = (r.xh2[s, :] * r.sm[0:1, :] + r.sm[1:2, :]).astype(bf16)

    over_rows(r.x.shape[0], rows, 256, 1)


def masks(r):
    length = r.docs.shape[1]
    same = iota((128, length), 0) == r.docs[...]
    r.kd[...] = jnp.where(same, 1.0, 0.0).T.astype(bf16)
    differ = jnp.logical_and(iota((128, length), 0) < 8, jnp.logical_not(same))
    r.qd[...] = jnp.where(differ, NEG, 0.0).astype(bf16)


def near_bias(r):
    for h in range(HEADS):
        by_dist = r.bd[h : h + 1, :]
        by_dist = by_dist - by_dist[:, 255:256]
        line = jnp.concatenate([jnp.full((1, TILE), NEG, f32), by_dist], axis=1)
        line = jnp.broadcast_to(line, (TILE, 3 * TILE))
        line = pltpu.roll(line, 0, 1, stride=1, stride_axis=0)
        half = slice((h % 2) * TILE, (h % 2 + 1) * TILE)
        r.near[h // 2, 0:TILE, half] = line[:, 2 * TILE :]
        r.near[h // 2, TILE:, half] = line[:, TILE : 2 * TILE]


def project(r, half):
    def rows(s):
        out = dot_nn(r.na[s, :], r.WH[half][:, 0 : 3 * HALF])
        q = (out[:, :HALF].astype(bf16) * bf16(HEAD_DIM**-0.5)).T
        k = out[:, HALF : 2 * HALF].astype(bf16)
        v = out[:, 2 * HALF :].astype(bf16)
        for j in range(2):
            lanes = slice(j * 128, (j + 1) * 128)
            r.qt[2 * half + j, :, s] = q[lanes, :]
            r.k[2 * half + j, s, :] = k[:, lanes]
            r.v[2 * half + j, s, :] = v[:, lanes]

    over_rows(r.x.shape[0], rows)


def bands(length):
    first = 0
    for b in range(length // TILE):
        low = max(0, b - LONGEST // TILE)
        count = (b + 1 - low) * TILE
        yield b, slice(low * TILE, (b + 1) * TILE), slice(b * TILE, (b + 1) * TILE), first, count
        first += count


def band_rows(length):
    return sum(count for _, _, _, _, count in bands(length))


def attend_forward(r, p):
    near = r.near[p]
    lanes = pl.ds(pl.multiple_of(p * 128, 128), 128)
    plan = list(bands(r.x.shape[0]))

    def scores(b, ks, qs, first, count):
        qd = r.qd[:, qs]
        rhs = jnp.concatenate(
            [split_heads(r.qt[p, :, qs]), jnp.concatenate([qd, qd], axis=1)], axis=0
        )
        lhs = jnp.concatenate([r.k[p, ks, :], r.kd[ks, :]], axis=1)
        st = dot_nn(lhs, rhs)
        if count > 2 * TILE:
            return jnp.concatenate([st[: count - 2 * TILE], st[count - 2 * TILE :] + near], axis=0)
        return st + near[2 * TILE - count :]

    def soften(st, b, first, count):
        lifted = jnp.exp(st - jnp.max(st, axis=0, keepdims=True))
        inverse = 1.0 / jnp.sum(lifted, axis=0, keepdims=True)
        weights = lifted.astype(bf16)
        r.P[p, first : first + count, :] = weights
        r.inv[p, b : b + 1, :] = inverse
        return weights, inverse

    def attended(weights, inverse, ks, qs):
        ot = join_heads(dot_tn(r.v[p, ks, :], weights) * inverse)
        r.ot[p, :, qs] = ot
        r.att[qs, lanes] = ot.T.astype(bf16)

    AHEAD = 1
    queue, soft = [], []
    steps = len(plan)
    for i in range(steps + 2):
        if i < steps:
            queue.append(scores(*plan[i]))
        if 1 <= i <= steps:
            b, ks, qs, first, count = plan[i - 1]
            soft.append(soften(queue.pop(0), b, first, count))
        if 2 <= i:
            b, ks, qs, first, count = plan[i - 2]
            attended(*soft.pop(0), ks, qs)


def attend_backward(r, p):
    length = r.x.shape[0]
    r.dk[...] = jnp.zeros_like(r.dk)
    r.dv[...] = jnp.zeros_like(r.dv)
    r.acc[...] = jnp.zeros_like(r.acc)
    inner = pl.multiple_of((p // 2) * 3 * HALF + (p % 2) * 128, 128)
    top = iota((128, TILE), 0) < HEAD_DIM
    plan = list(bands(length))

    def soft_grad(b, ks, qs, first, count):
        inverse = r.inv[p, b : b + 1, :]
        scale = jnp.where(top, inverse[:, :TILE], inverse[:, TILE:])
        dot_ = (r.dot[p, :, qs].astype(f32) * scale).astype(bf16)
        prod = dot_.astype(f32) * r.ot[p, :, qs]
        delta = jnp.concatenate(
            [
                jnp.sum(prod[:HEAD_DIM], axis=0, keepdims=True),
                jnp.sum(prod[HEAD_DIM:], axis=0, keepdims=True),
            ],
            axis=1,
        )
        dcat = split_heads(dot_)
        return dcat, delta, dot_nn(r.v[p, ks, :], dcat)

    def score_grad(dcat, delta, dpt, first, count):
        weights = r.P[p, first : first + count, :]
        ds = weights.astype(f32) * (dpt - delta)
        if count >= 2 * TILE:
            r.acc[...] += ds[count - 2 * TILE :]
        else:
            r.acc[TILE:, :] += ds
        return weights, dcat, ds.astype(bf16)

    def operand_grads(weights, dcat, dsb, ks, qs):
        r.dv[ks, :] += dot_nt(weights, dcat)
        r.dk[ks, :] += dot_nt(dsb, split_heads(r.qt[p, :, qs]))
        dqt = join_heads(dot_tn(r.k[p, ks, :], dsb)) * HEAD_DIM**-0.5
        r.gh[qs, pl.ds(inner, 128)] = dqt.T.astype(bf16)

    soft, score = [], []
    steps = len(plan)
    for i in range(steps + 2):
        if i < steps:
            soft.append(soft_grad(*plan[i]))
        if 1 <= i <= steps:
            b, ks, qs, first, count = plan[i - 1]
            score.append(score_grad(*soft.pop(0), first, count))
        if 2 <= i:
            b, ks, qs, first, count = plan[i - 2]
            operand_grads(*score.pop(0), ks, qs)
    r.gh[:, pl.ds(HALF + inner, 128)] = r.dk[...].astype(bf16)
    r.gh[:, pl.ds(2 * HALF + inner, 128)] = r.dv[...].astype(bf16)
    zero = jnp.zeros((TILE, TILE), f32)
    rows = iota((TILE, 3 * TILE), 0)
    for h in range(2):
        half = slice(h * TILE, (h + 1) * TILE)
        line = jnp.concatenate([zero, r.acc[TILE:, half], r.acc[:TILE, half]], axis=1)
        for bit in range(7):
            rolled = pltpu.roll(line, 3 * TILE - (1 << bit), 1)
            line = jnp.where((rows >> bit) & 1 == 1, rolled, line)
        r.lines[pl.ds(2 * p + h, 1), :] = jnp.sum(line, axis=0, keepdims=True)


def table_grad(r):
    by_dist = r.lines[:, TILE:]
    dist = iota((2 * TILE, 128), 0)
    near = jnp.logical_and(bucket_of(dist) == iota((2 * TILE, 128), 1), dist < 2 * TILE)
    near = jnp.logical_and(near, iota((2 * TILE, 128), 1) < BUCKETS - 1)
    counted = lax.dot_general(
        by_dist,
        jnp.where(near, 1.0, 0.0),
        (((1,), (0,)), ((), ())),
        precision=lax.Precision.HIGHEST,
        preferred_element_type=f32,
    )
    rest = -jnp.sum(counted, axis=1, keepdims=True)
    r.tg[...] = jnp.where(iota((HEADS, 128), 1) == BUCKETS - 1, rest, counted)


def before_ff(r):
    r.smg[...] = jnp.zeros_like(r.smg)
    r.esg[...] = jnp.zeros_like(r.esg)

    def rows(s):
        residual = r.x[s, :].astype(f32) + dot_nn(r.att[s, :], r.WO[...]) + r.sm[2:3, :]
        xh, rstd = standardize(residual)
        r.xh2[s, :] = xh
        r.rstd2[s, :] = rstd
        r.nf[s, :] = (xh * r.sm[3:4, :] + r.sm[4:5, :]).astype(bf16)
        r.branch[s, :] = residual + r.sm[5:6, :]

    over_rows(r.x.shape[0], rows)


def feed_forward(r, f):
    cols = slice(f * WIDE, (f + 1) * WIDE)
    half = r.W1[f // 2]
    inner = slice((f % 2) * WIDE, (f % 2 + 1) * WIDE)

    def rows(s):
        hidden = dot_nn(r.nf[s, :], half[:, inner]) + r.es[0:1, cols]
        active, slope = gelu_parts(hidden)
        r.act[s, cols] = active.astype(bf16)
        r.gh[s, cols] = slope.astype(bf16)

    over_rows(r.x.shape[0], rows, 256, 4)


def feed_backward(r, f):
    cols = slice(f * WIDE, (f + 1) * WIDE)

    def rows(s):
        gh = dot_nt(r.g[s, :], r.W2[cols, :]) * r.gh[s, cols].astype(f32)
        r.esg[0:1, cols] += jnp.sum(gh, axis=0, keepdims=True)
        r.gh[s, cols] = gh.astype(bf16)

    over_rows(r.x.shape[0], rows)


def after_ff(r, s):
    ff = r.es.shape[1]
    gnf = dot_nt(r.gh[s, : ff // 2], r.W1[0][...]) + dot_nt(r.gh[s, ff // 2 :], r.W1[1][...])
    xh = r.xh2[s, :]
    gf = r.g[s, :].astype(f32)
    grad = gf + standardize_back(gnf * r.sm[3:4, :], xh, r.rstd2[s, :])
    r.xh2[s, :] = grad
    gb = grad.astype(bf16)
    r.gb[s, :] = gb
    r.smg[2:3, :] += jnp.sum(gb.astype(f32), axis=0, keepdims=True)
    r.smg[3:4, :] += jnp.sum(gnf * xh, axis=0, keepdims=True)
    r.smg[4:5, :] += jnp.sum(gnf, axis=0, keepdims=True)
    r.smg[5:6, :] += jnp.sum(gf, axis=0, keepdims=True)
    dot_ = dot_nt(gb, r.WO[...]).astype(bf16).T
    for p in range(PAIRS):
        r.dot[p, :, s] = dot_[p * 128 : (p + 1) * 128, :]


def output(r, s):
    r.nf[s, :] = (r.branch[s, :] + dot_nn(r.act[s, :], r.W2[...])).astype(bf16)


def half_columns(half):
    return slice(half * 3 * HALF, (half + 1) * 3 * HALF)


def pair_columns(ref, rows, p, base=0):
    at = base + (p % 2) * 128
    return jnp.concatenate(
        [ref[rows, part * HALF + at : part * HALF + at + 128] for part in range(3)], axis=1
    )


def back_project(r, half, pair=None):
    def rows(s):
        if pair is None:
            grads, weight = r.gh[s, half_columns(half)], r.WH[half][:, 0 : 3 * HALF]
        else:
            grads = pair_columns(r.gh, s, pair, half * 3 * HALF)
            weight = pair_columns(r.WH[half], slice(None), pair)
        part = dot_nt(grads, weight)
        r.gnf[s, :] = part if half == 0 else r.gnf[s, :] + part

    over_rows(r.x.shape[0], rows)


def last(r):
    def rows(s):
        gna = r.gnf[s, :]
        xh, rstd = standardize(r.x[s, :].astype(f32))
        r.xh2[s, :] += standardize_back(gna * r.sm[0:1, :], xh, rstd)
        r.smg[0:1, :] += jnp.sum(gna * xh, axis=0, keepdims=True)
        r.smg[1:2, :] += jnp.sum(gna, axis=0, keepdims=True)

    over_rows(r.x.shape[0], rows)


def weight_grad(left, right, step, put):
    count = left.shape[1] // step
    if count == 1:
        put(0, dot_tn(left[...], right()))
        return

    def rows(i, c):
        put(i, dot_tn(left[:, pl.ds(pl.multiple_of(i * step, step), step)], right()))
        return c

    lax.fori_loop(0, count, rows, 0)


class Place:
    def __init__(self, dp_size, fsdp_size):
        dp, x = lax.axis_index("dp"), lax.axis_index("fsdp")
        self.z, self.y, self.c, self.x = dp // 4, (dp // 2) % 2, dp % 2, x
        self.zs = dp_size // 4

    def zpeer(self, m):
        z = self.z
        return (z, z + 1 - 2 * (z % 2), (z + 2) % 4, 3 - z)[m]

    def index(self, m, t, other=False):
        x = 1 - self.x if t in (1, 3) else self.x
        y = 1 - self.y if t in (2, 3) else self.y
        c = 1 - self.c if other else self.c
        return ((self.zpeer(m) * 2 + y) * 2 + c) * 2 + x

    def inner(self, t, other=False):
        x = 1 - self.x if t in (1, 3) else self.x
        y = 1 - self.y if t in (2, 3) else self.y
        c = 1 - self.c if other else self.c
        return (y * 2 + c) * 2 + x

    def device(self, m=0, t=0, other=False):
        x = 1 - self.x if t in (1, 3) else self.x
        y = 1 - self.y if t in (2, 3) else self.y
        c = 1 - self.c if other else self.c
        return ((self.zpeer(m) * 2 + y) * 2 + c, x)

    def neighbours(self):
        return [self.device(m=m) for m in (1, 2, 3)] + [
            self.device(t=1),
            self.device(t=2),
            self.device(t=3),
            self.device(other=True),
        ]


def greet(place):
    barrier = pltpu.get_barrier_semaphore()
    for peer in place.neighbours():
        pl.semaphore_signal(
            barrier, inc=1, device_id=peer, device_id_type=pl.DeviceIdType.MESH
        )


def enter():
    pl.semaphore_wait(pltpu.get_barrier_semaphore(), 7)


GATHER_SEMS, SCATTER_SEMS = 8, 9
X, Y, OPPOSITE_A, OPPOSITE_B, SIBLING = 3, 4, 5, 6, 7


class Gather:
    def __init__(self, place, whole, rho, half, send, recv):
        self.place, self.whole, self.rho, self.half = place, whole, rho, half
        self.send, self.recv = send, recv

    def view(self, shard, part=None, count=1):
        rows = pl.ds(pl.multiple_of(shard * self.rho, 16), count * self.rho)
        if part is None:
            return self.whole.at[rows, :]
        cols = slice(0, self.half) if part == 0 else slice(self.half, self.whole.shape[1])
        return self.whole.at[rows, cols]

    def copy(self, ref, sem, device):
        return pltpu.make_async_remote_copy(
            src_ref=ref,
            dst_ref=ref,
            send_sem=self.send,
            recv_sem=self.recv.at[sem],
            device_id=device,
            device_id_type=pl.DeviceIdType.MESH,
        )

    def start(self, shard, sem, device, part=None):
        self.copy(self.view(shard, part), sem, device).start()

    def arrive(self, count, sem, part=None):
        ref = self.view(0, part, count)
        self.copy(ref, sem, self.place.device(other=True)).wait_recv()

    def along_z(self):
        at = self.place
        for m in (1, 2, 3):
            self.start(at.index(0, 0), m - 1, at.device(m=m))

    def first(self):
        self.along_z()
        self.spread(0)

    def spread(self, m):
        at = self.place
        shard = at.index(m, 0)
        self.start(shard, X, at.device(t=1))
        self.start(shard, Y, at.device(t=2))
        if self.half is None:
            self.start(shard, OPPOSITE_A, at.device(t=3))
        self.start(shard, SIBLING, at.device(other=True))

    def second(self):
        for m in (1, 2, 3):
            self.arrive(1, m - 1)
            self.spread(m)

    def third(self):
        at = self.place
        self.arrive(4, X)
        for m in range(4):
            if self.half is not None:
                self.start(at.index(m, 1), OPPOSITE_A, at.device(t=2), 0)
        for m in range(4):
            self.start(at.index(m, 1), SIBLING, at.device(other=True))
        self.arrive(4, Y)
        for m in range(4):
            if self.half is not None:
                self.start(at.index(m, 2), OPPOSITE_B, at.device(t=1), 1)
        for m in range(4):
            self.start(at.index(m, 2), SIBLING, at.device(other=True))

    def fourth(self):
        at = self.place
        if self.half is None:
            self.arrive(4, OPPOSITE_A)
        else:
            self.arrive(4, OPPOSITE_A, 0)
            self.arrive(4, OPPOSITE_B, 1)
        for m in range(4):
            self.start(at.index(m, 3), SIBLING, at.device(other=True))

    def finish(self):
        self.arrive(16, SIBLING)

    def drain(self):
        self.copy(self.view(0, None, 31), X, self.place.device(other=True)).wait_send()


class Scatter:
    def __init__(self, place, full, bufs, half, send, recv, emit):
        self.place, self.full, self.half, self.emit = place, full, half, emit
        self.sib, self.ra, self.rb, self.rx, self.ry, self.rz = bufs
        self.send, self.recv = send, recv

    def copy(self, src, dst, sem, device):
        group = 0 if sem < 4 else 1 if sem < 8 else 2
        return pltpu.make_async_remote_copy(
            src_ref=src,
            dst_ref=dst,
            send_sem=self.send.at[group],
            recv_sem=self.recv.at[sem],
            device_id=device,
            device_id_type=pl.DeviceIdType.MESH,
        )

    def start(self, src, dst, sem, device):
        self.copy(src, dst, sem, device).start()

    def arrive(self, dst, sem):
        self.copy(dst, dst, sem, self.place.device(other=True)).wait_recv()

    def first(self):
        at = self.place
        for t in (3, 1, 2, 0):
            self.start(
                self.full.at[:, at.inner(t, other=True)], self.sib.at[t], t, at.device(other=True)
            )

    def merge(self, t):
        self.arrive(self.sib.at[t], t)
        self.sib[t] += self.full[:, self.place.inner(t)]

    def second(self):
        at = self.place
        self.merge(3)
        if self.half is None:
            self.start(self.sib.at[3], self.ra, 4, at.device(t=3))
            self.merge(1)
            self.start(self.sib.at[1], self.rx, 6, at.device(t=1))
            self.merge(2)
            self.start(self.sib.at[2], self.ry, 7, at.device(t=2))
        else:
            self.start(self.sib.at[3, :, :, : self.half], self.ra, 4, at.device(t=1))
            self.start(self.sib.at[3, :, :, self.half :], self.rb, 5, at.device(t=2))

    def third(self):
        at = self.place
        if self.half is None:
            return
        self.merge(1)
        self.merge(2)
        self.arrive(self.rb, 5)
        self.sib[1, :, :, self.half :] += self.rb[...]
        self.start(self.sib.at[1], self.rx, 6, at.device(t=1))
        self.arrive(self.ra, 4)
        self.sib[2, :, :, : self.half] += self.ra[...]
        self.start(self.sib.at[2], self.ry, 7, at.device(t=2))

    def fourth(self):
        at = self.place
        self.merge(0)
        self.arrive(self.rx, 6)
        self.arrive(self.ry, 7)
        total = self.rx[...].astype(f32) + self.ry[...].astype(f32)
        if self.half is None:
            self.arrive(self.ra, 4)
            total = total + self.ra[...].astype(f32)
        self.sib[0] += total.astype(bf16)
        for m in (1, 2, 3):
            self.start(self.sib.at[0, at.zpeer(m)], self.rz.at[m - 1], 8, at.device(m=m))

    def fifth(self):
        self.arrive(self.rz, 8)
        total = self.sib[0, self.place.z].astype(f32)
        for m in (1, 2, 3):
            total = total + self.rz[m - 1].astype(f32)
        self.emit(total)

    def drain(self):
        for sem, ref in ((0, self.sib), (4, self.sib.at[0:3]), (8, self.rz)):
            self.copy(ref, ref, sem, self.place.device(other=True)).wait_send()


class ScatterByPlane(Scatter):
    def copy(self, src, dst, sem, device):
        group = 0 if sem < 16 else 1 if sem < 32 else 2
        return pltpu.make_async_remote_copy(
            src_ref=src,
            dst_ref=dst,
            send_sem=self.send.at[group],
            recv_sem=self.recv.at[sem],
            device_id=device,
            device_id_type=pl.DeviceIdType.MESH,
        )

    def first(self, z):
        at = self.place
        for t in (3, 1, 2, 0):
            self.start(
                self.full.at[z, at.inner(t, other=True)],
                self.sib.at[t, z],
                4 * t + z,
                at.device(other=True),
            )

    def merge(self, t, z):
        self.arrive(self.sib.at[t, z], 4 * t + z)
        self.sib[t, z] += self.full[z, self.place.inner(t)]

    def second(self, z):
        at = self.place
        self.merge(3, z)
        self.start(self.sib.at[3, z, :, : self.half], self.ra.at[z], 16 + z, at.device(t=1))
        self.start(self.sib.at[3, z, :, self.half :], self.rb.at[z], 20 + z, at.device(t=2))

    def third(self, z):
        at = self.place
        self.merge(1, z)
        self.merge(2, z)
        self.arrive(self.rb.at[z], 20 + z)
        self.sib[1, z, :, self.half :] += self.rb[z]
        self.start(self.sib.at[1, z], self.rx.at[z], 24 + z, at.device(t=1))
        self.arrive(self.ra.at[z], 16 + z)
        self.sib[2, z, :, : self.half] += self.ra[z]
        self.start(self.sib.at[2, z], self.ry.at[z], 28 + z, at.device(t=2))

    def fourth(self):
        at = self.place
        for z in range(4):
            self.merge(0, z)
            self.arrive(self.rx.at[z], 24 + z)
            self.arrive(self.ry.at[z], 28 + z)
            total = self.rx[z].astype(f32) + self.ry[z].astype(f32)
            self.sib[0, z] += total.astype(bf16)
        for m in (1, 2, 3):
            self.start(self.sib.at[0, at.zpeer(m)], self.rz.at[m - 1], 32, at.device(m=m))

    def fifth(self):
        self.arrive(self.rz, 32)
        total = self.sib[0, self.place.z].astype(f32)
        for m in (1, 2, 3):
            total = total + self.rz[m - 1].astype(f32)
        self.emit(total)

    def drain(self):
        for sem, ref in ((0, self.sib), (16, self.sib.at[0:3]), (32, self.rz)):
            self.copy(ref, ref, sem, self.place.device(other=True)).wait_send()


def scatter_bufs(rho, cols, half):
    first = cols if half is None else half
    rest = 128 if half is None else cols - half
    return [
        pltpu.VMEM((4, 4, rho, cols), bf16),
        pltpu.VMEM((4, rho, first), bf16),
        pltpu.VMEM((4, rho, rest), bf16),
        pltpu.VMEM((4, rho, cols), bf16),
        pltpu.VMEM((4, rho, cols), bf16),
        pltpu.VMEM((3, rho, cols), bf16),
    ]


def over_pairs(attend, r, first, end, pump):
    def one(p, c):
        attend(r, p)
        for pair in range(first, end):
            if pair in pump:

                @pl.when(p == pair)
                def _():
                    pump[pair]()
        return c

    lax.fori_loop(first, end, one, 0)


def work_scratch(length, ff):
    tokens = band_rows(length)
    return dict(
        x=pltpu.VMEM((length, D), bf16),
        na=pltpu.VMEM((length, D), bf16),
        kd=pltpu.VMEM((length, 128), bf16),
        qd=pltpu.VMEM((128, length), bf16),
        near=pltpu.VMEM((PAIRS, 2 * TILE, 2 * TILE), f32),
        qt=pltpu.VMEM((PAIRS, 128, length), bf16),
        k=pltpu.VMEM((PAIRS, length, 128), bf16),
        v=pltpu.VMEM((PAIRS, length, 128), bf16),
        P=pltpu.VMEM((PAIRS, tokens, 2 * TILE), bf16),
        inv=pltpu.VMEM((PAIRS, length // TILE, 2 * TILE), f32),
        ot=pltpu.VMEM((PAIRS, 128, length), f32),
        att=pltpu.VMEM((length, D), bf16),
        xh2=pltpu.VMEM((length, D), f32),
        rstd2=pltpu.VMEM((length, 1), f32),
        branch=pltpu.VMEM((length, D), f32),
        gnf=pltpu.VMEM((length, D), f32),
        nf=pltpu.VMEM((length, D), bf16),
        act=pltpu.VMEM((length, ff), bf16),
        gh=pltpu.VMEM((length, ff), bf16),
        gb=pltpu.VMEM((length, D), bf16),
        dot=pltpu.VMEM((PAIRS, 128, length), bf16),
        dk=pltpu.VMEM((length, 128), f32),
        dv=pltpu.VMEM((length, 128), f32),
        acc=pltpu.VMEM((2 * TILE, 2 * TILE), f32),
        lines=pltpu.VMEM((HEADS, 3 * TILE), f32),
    )


def small_scratch(ff):
    return dict(
        sm=pltpu.VMEM((16, D), f32),
        es=pltpu.VMEM((8, ff), f32),
        bd=pltpu.VMEM((HEADS, 256), f32),
        smg=pltpu.VMEM((16, D), f32),
        esg=pltpu.VMEM((8, ff), f32),
        tg=pltpu.VMEM((HEADS, 128), f32),
    )


def run_kernel(kernel, operands, out_shape, scratch, in_hbm=(), out_hbm=(), **params):
    names = list(scratch)
    count = len(operands) + len(out_shape)

    def named(*refs):
        kernel(refs[: len(operands)], refs[len(operands) : count], dict(zip(names, refs[count:])))

    def specs(number, hbm):
        return [
            pl.BlockSpec(memory_space=pl.ANY if i in hbm else pltpu.VMEM) for i in range(number)
        ]

    return pl.pallas_call(
        named,
        out_shape=out_shape,
        in_specs=specs(len(operands), in_hbm),
        out_specs=specs(len(out_shape), out_hbm),
        scratch_shapes=[scratch[name] for name in names],
        compiler_params=pltpu.CompilerParams(vmem_limit_bytes=VMEM_BYTES, **params),
    )(*operands)


VMEM_BYTES = 63 * 1024 * 1024


def whole_layer(x, documents, g, small, w_a, w_o, w_1, w_2, dp_size, fsdp_size):
    n = dp_size * fsdp_size
    length, ff = x.shape[0], w_1.shape[1]
    ra, r2 = w_1.shape[0], w_2.shape[0]
    gathered = dict(
        H0=(ra, 3 * HALF + 128, None),
        H1=(ra, 3 * HALF, None),
        WO=(ra, D, HALF),
        W2=(r2, D, HALF),
        W1a=(ra, ff // 2, ff // 4),
        W1b=(ra, ff // 2, ff // 4),
    )
    scattered = dict(
        d1a=(ra, ff // 2, ff // 4),
        d1b=(ra, ff // 2, ff // 4),
        d2=(r2, D, HALF),
        dO=(ra, D, HALF),
        dH=(ra, 3 * HALF, HALF),
        dT2=(ra, 384, 128),
        dT3=(ra, 384, None),
        dS=(ra, 128, None),
    )
    scratch = dict(work_scratch(length, ff), **small_scratch(ff))
    scratch["g"] = pltpu.VMEM((length, D), bf16)
    for name, (rho, cols, _) in gathered.items():
        scratch[name] = pltpu.VMEM((n * rho, cols), bf16)
    for name, (rho, cols, half) in scattered.items():
        scratch[name] = pltpu.VMEM((4, 8, rho, cols), bf16)
        for j, buf in enumerate(scatter_bufs(rho, cols, half)):
            scratch["%s_%d" % (name, j)] = buf
    dma = pltpu.SemaphoreType.DMA
    scratch.update(
        gsend=dma((len(gathered),)),
        grecv=dma((len(gathered), GATHER_SEMS)),
        prec=dma((33,)),
        ssend=dma((len(scattered), 3)),
        srecv=dma((len(scattered), SCATTER_SEMS)),
        move=dma((4,)),
    )

    def kernel(ins, outs, s):
        r = types.SimpleNamespace(**s)
        x_in, r.docs, g_in = ins[:3]
        vectors, (own_a, own_o, own_1, own_2) = ins[3:11], ins[11:]
        out, igrad, out_a, out_o, out_1, out_2, out_s = outs
        r.WH, r.W1 = [r.H0, r.H1], [r.W1a, r.W1b]
        at = Place(dp_size, fsdp_size)
        get_x = pltpu.make_async_copy(x_in, r.x, r.move.at[0])
        get_g = pltpu.make_async_copy(g_in, r.g, r.move.at[1])
        put_out = pltpu.make_async_copy(r.nf, out, r.move.at[2])
        put_igrad = pltpu.make_async_copy(r.xh2, igrad, r.move.at[3])
        get_x.start()
        get_g.start()
        greet(at)
        mine = at.index(0, 0)
        rows_a = pl.ds(pl.multiple_of(mine * ra, 16), ra)
        rows_2 = pl.ds(pl.multiple_of(mine * r2, 16), r2)
        for half, ref in enumerate(r.WH):
            for part in range(3):
                ref[rows_a, part * HALF : (part + 1) * HALF] = own_a[
                    :, part * D + half * HALF : part * D + (half + 1) * HALF
                ]
        lines = [
            jnp.concatenate(
                [v[...].astype(f32), jnp.zeros((1, 128 - v.shape[1]), f32)], axis=1
            )
            for v in vectors
        ]
        lines.append(jnp.zeros((ra - len(lines), 128), f32))
        r.H0[rows_a, 3 * HALF :] = jnp.concatenate(lines, axis=0).astype(bf16)
        r.WO[rows_a, :] = own_o[...]
        r.W2[rows_2, :] = own_2[...]
        for half, ref in enumerate(r.W1):
            ref[rows_a, :] = own_1[:, half * ff // 2 : (half + 1) * ff // 2]
        gathers = {
            name: Gather(at, s[name], rho, half, r.gsend.at[i], r.grecv.at[i])
            for i, (name, (rho, _, half)) in enumerate(gathered.items())
        }
        h0, h1, wo, w2, w1a, w1b = gathers.values()
        enter()
        h0.first()
        masks(r)
        get_x.wait()
        standardize_first(r)
        h0.second()
        h1.first()
        wo.first()
        h0.third()
        h0.fourth()
        h0.finish()
        unpack_small(r, n)
        norm_first(r)
        h1.second()
        w1a.first()
        near_bias(r)
        wo.second()
        project(r, 0)
        w1b.first()
        h1.third()
        w1a.second()

        def pump_0():
            h1.fourth()
            wo.third()
            w2.first()

        def pump_1():
            w1a.third()
            w1b.second()
            h1.finish()

        def pump_2():
            wo.fourth()
            w2.second()

        def pump_3():
            w1a.fourth()
            w1b.third()
            wo.finish()

        over_pairs(attend_forward, r, 0, 2, {0: pump_0, 1: pump_1})
        project(r, 1)
        over_pairs(attend_forward, r, 2, 4, {2: pump_2, 3: pump_3})
        unpack_expand_shift(r, n)
        before_ff(r)
        w1a.finish()
        get_g.wait()

        def emit_into(ref, cols):
            def emit(total):
                ref[:, cols] = total

            return emit

        def emit_pairs(pairs):
            def emit(total):
                wide = 128 * len(pairs)
                for part in range(3):
                    first = part * D + pairs[0] * 128
                    out_a[:, first : first + wide] = total[:, part * wide : (part + 1) * wide]

            return emit

        emits = dict(
            d1a=emit_into(out_1, slice(0, ff // 2)),
            d1b=emit_into(out_1, slice(ff // 2, ff)),
            d2=emit_into(out_2, slice(None)),
            dO=emit_into(out_o, slice(None)),
            dH=emit_pairs((0, 1)),
            dT2=emit_pairs((2,)),
            dT3=emit_pairs((3,)),
            dS=emit_into(out_s, slice(None)),
        )
        scatters = {
            name: (ScatterByPlane if name == "d2" else Scatter)(
                at,
                s[name],
                [s["%s_%d" % (name, j)] for j in range(6)],
                half,
                r.ssend.at[i],
                r.prec if name == "d2" else r.srecv.at[i],
                emits[name],
            )
            for i, (name, (_, _, half)) in enumerate(scattered.items())
        }
        s1a, s1b, s2, so, sh, st2, st3, ss = scatters.values()

        def put_shards(ref, step, rho, first=0):
            count = step // (8 * rho)

            def put(i, value):
                value = value.astype(bf16).reshape(count, 8, rho, value.shape[1])
                ref[pl.ds(count * i, count), :, :, first : first + value.shape[3]] = value

            return put

        def expand_grad(f, ref):
            cols = slice(f * WIDE, (f + 1) * WIDE)
            weight_grad(
                r.nf, lambda: r.gh[:, cols], D, put_shards(ref, D, ra, (f % 2) * WIDE)
            )

        def reduce_grad(f):
            act = r.act[:, f * WIDE : (f + 1) * WIDE]
            r.d2[f] = dot_tn(act, r.g[...]).astype(bf16).reshape(8, r2, D)
            s2.first(f)

        feed_forward(r, 0)
        reduce_grad(0)
        w1b.fourth()
        feed_forward(r, 1)
        reduce_grad(1)
        s2.second(0)
        w1b.finish()
        w2.third()
        feed_forward(r, 2)
        reduce_grad(2)
        s2.second(1)
        feed_forward(r, 3)
        reduce_grad(3)
        s2.third(0)
        s2.second(2)
        w2.fourth()
        s2.third(1)
        w2.finish()
        feed_backward(r, 0)
        expand_grad(0, r.d1a)
        s2.second(3)
        feed_backward(r, 1)
        expand_grad(1, r.d1a)
        s1a.first()
        s2.third(2)
        feed_backward(r, 2)
        expand_grad(2, r.d1b)
        s2.third(3)
        feed_backward(r, 3)
        expand_grad(3, r.d1b)
        s1b.first()
        s1a.second()
        after_ff(r, slice(0, BLOCK))
        s2.fourth()
        for i in range(1, length // BLOCK):
            after_ff(r, slice(i * BLOCK, (i + 1) * BLOCK))
        s1b.second()
        s1a.third()
        weight_grad(r.att, lambda: r.gb[...], D, put_shards(r.dO, D, ra))
        so.first()

        def pump_0():
            so.second()
            s1b.third()

        def pump_1():
            s2.fifth()
            s1a.fourth()
            so.third()

        def pump_2():
            sh.second()
            s1b.fourth()
            so.fourth()

        def pump_3():
            st2.second()
            sh.third()
            s1a.fifth()

        pump = {0: pump_0, 1: pump_1, 2: pump_2, 3: pump_3}
        over_pairs(attend_backward, r, 0, 2, pump)
        weight_grad(
            r.na, lambda: r.gh[:, half_columns(0)], D, put_shards(r.dH, D, ra)
        )
        sh.first()
        back_project(r, 0)
        over_pairs(attend_backward, r, 2, 3, pump)
        weight_grad(
            r.na, lambda: pair_columns(r.gh, slice(None), 2, 3 * HALF), D, put_shards(r.dT2, D, ra)
        )
        st2.first()
        back_project(r, 1, 2)
        over_pairs(attend_backward, r, 3, 4, pump)
        weight_grad(
            r.na, lambda: pair_columns(r.gh, slice(None), 3, 3 * HALF), D, put_shards(r.dT3, D, ra)
        )
        st3.first()
        back_project(r, 1, 3)
        last(r)
        put_igrad.start()
        st3.second()
        table_grad(r)
        r.dS[...] = pack_small_grads(r, n).astype(bf16).reshape(4, 8, ra, 128)
        ss.first()
        sh.fourth()
        st2.third()
        output(r, slice(0, BLOCK))
        ss.second()
        for i in range(1, length // BLOCK):
            output(r, slice(i * BLOCK, (i + 1) * BLOCK))
        put_out.start()
        s1b.fifth()
        so.fifth()
        st3.fourth()
        st2.fourth()
        ss.fourth()
        sh.fifth()
        st3.fifth()
        st2.fifth()
        ss.fifth()
        for item in list(gathers.values()) + list(scatters.values()):
            item.drain()
        put_out.wait()
        put_igrad.wait()

    out_shape = [
        jax.ShapeDtypeStruct((length, D), bf16),
        jax.ShapeDtypeStruct((length, D), f32),
        jax.ShapeDtypeStruct((ra, 3 * D), f32),
        jax.ShapeDtypeStruct((ra, D), f32),
        jax.ShapeDtypeStruct((ra, ff), f32),
        jax.ShapeDtypeStruct((r2, D), f32),
        jax.ShapeDtypeStruct((ra, 128), f32),
    ]
    operands = [x, documents, g, *small, w_a, w_o, w_1, w_2]
    return run_kernel(
        kernel,
        operands,
        out_shape,
        scratch,
        in_hbm=(0, 2),
        out_hbm=(0, 1),
        collective_id=0,
        has_side_effects=True,
    )


def hand_out(results, sizes):
    length = results[0].shape[0]
    pieces = 4
    chunk = length // pieces

    def kernel(ins, outs, s):
        buffers = (s["a"], s["b"])

        def move(i, j, back):
            rows = slice(j * chunk, (j + 1) * chunk)
            here = buffers[i].at[rows, :]
            there = (outs if back else ins)[i].at[rows, :]
            sem = s["move"].at[pieces * i + j, int(back)]
            if back:
                return pltpu.make_async_copy(here, there, sem)
            return pltpu.make_async_copy(there, here, sem)

        parts = [(i, j) for j in range(pieces) for i in range(2)]
        for i, j in parts:
            move(i, j, False).start()
        for i in range(2, 6):
            outs[i][...] = ins[i][...]
        for i, size in enumerate(sizes):
            outs[6 + i][...] = ins[6][i : i + 1, :size]
        for i, j in parts:
            move(i, j, False).wait()
            move(i, j, True).start()
        for i, j in parts:
            move(i, j, True).wait()

    out_shape = [jax.ShapeDtypeStruct(v.shape, v.dtype) for v in results[:6]]
    out_shape += [jax.ShapeDtypeStruct((1, size), f32) for size in sizes]
    scratch = dict(
        a=pltpu.VMEM(results[0].shape, results[0].dtype),
        b=pltpu.VMEM(results[1].shape, results[1].dtype),
        move=pltpu.SemaphoreType.DMA((2 * pieces, 2)),
    )
    return run_kernel(
        kernel, list(results), out_shape, scratch, in_hbm=(0, 1), out_hbm=(0, 1)
    )


def local_layer(x, documents, g, h0, h1, w_o, w_1a, w_1b, w_2, sm, es, bd):
    length, ff = x.shape[0], 2 * w_1a.shape[1]
    scratch = dict(work_scratch(length, ff))

    def kernel(ins, outs, s):
        r = types.SimpleNamespace(**s)
        x_in, r.docs, r.g, h0_, h1_, r.WO, w1a_, w1b_, r.W2, r.sm, r.es, r.bd = ins
        out, igrad, d_a, d_o, d_1, d_2, r.smg, r.esg, r.tg = outs
        r.WH, r.W1 = [h0_, h1_], [w1a_, w1b_]
        r.x[...] = x_in[...]
        masks(r)
        near_bias(r)
        standardize_first(r)
        norm_first(r)
        project(r, 0)
        project(r, 1)

        over_pairs(attend_forward, r, 0, PAIRS, {})
        before_ff(r)

        def put_into(ref, step, first, wide):
            def put(i, value):
                rows = pl.ds(pl.multiple_of(i * step, step), step)
                ref[rows, first : first + wide] = value.astype(ref.dtype)

            return put

        for f in range(ff // WIDE):
            feed_forward(r, f)
        weight_grad(r.act, lambda: r.g[...], 1024, put_into(d_2, 1024, 0, D))
        for f in range(ff // WIDE):
            cols = slice(f * WIDE, (f + 1) * WIDE)
            feed_backward(r, f)
            weight_grad(
                r.nf, lambda cols=cols: r.gh[:, cols], D, put_into(d_1, D, f * WIDE, WIDE)
            )
        for i in range(length // BLOCK):
            after_ff(r, slice(i * BLOCK, (i + 1) * BLOCK))
        for i in range(length // BLOCK):
            output(r, slice(i * BLOCK, (i + 1) * BLOCK))
        out[...] = r.nf[...]
        weight_grad(r.att, lambda: r.gb[...], D, put_into(d_o, D, 0, D))
        over_pairs(attend_backward, r, 0, PAIRS, {})
        for half in range(2):
            back_project(r, half)

            def put(i, value, half=half):
                for part in range(3):
                    first = part * D + half * HALF
                    d_a[:, first : first + HALF] = value[
                        :, part * HALF : (part + 1) * HALF
                    ].astype(bf16)

            weight_grad(r.na, lambda half=half: r.gh[:, half_columns(half)], D, put)
        last(r)
        table_grad(r)
        igrad[...] = r.xh2[...]

    out_shape = [
        jax.ShapeDtypeStruct((length, D), bf16),
        jax.ShapeDtypeStruct((length, D), f32),
        jax.ShapeDtypeStruct((D, 3 * D), bf16),
        jax.ShapeDtypeStruct((D, D), bf16),
        jax.ShapeDtypeStruct((D, ff), bf16),
        jax.ShapeDtypeStruct((ff, D), bf16),
        jax.ShapeDtypeStruct((16, D), f32),
        jax.ShapeDtypeStruct((8, ff), f32),
        jax.ShapeDtypeStruct((HEADS, 128), f32),
    ]
    operands = [x, documents, g, h0, h1, w_o, w_1a, w_1b, w_2, sm, es, bd]
    return run_kernel(kernel, operands, out_shape, scratch)


def whole_body(dp_size, fsdp_size):
    def body(x, documents, fg, fs, w_a, table, w_o, os, sg, ss, w_1, es, w_2, rs, g):
        vectors = (fg, fs, os, sg, ss, rs, es, table)
        results = whole_layer(
            x,
            documents,
            g,
            [v.reshape(1, -1) for v in vectors],
            w_a,
            w_o,
            w_1,
            w_2,
            dp_size,
            fsdp_size,
        )
        out, igrad, d_a, d_o, d_1, d_2, *small = hand_out(
            results, [v.shape[0] for v in vectors]
        )
        dfg, dfs, dos, dsg, dss, drs, des, dtable = [v.reshape(-1) for v in small]
        return (out, igrad, dfg, dfs, d_a, dtable, d_o, dos, dsg, dss, d_1, des, d_2, drs)

    return body


def split_body(x, documents, fg, fs, w_a, table, w_o, os, sg, ss, w_1, es, w_2, rs, g):
    def whole(v):
        return lax.all_gather(v, AXES, axis=0, tiled=True)

    def mine(v):
        return lax.psum_scatter(v.astype(f32), AXES, scatter_dimension=0, tiled=True)

    parts = [w_a[:, i * HALF : (i + 1) * HALF] for i in range(6)]
    h0 = whole(jnp.concatenate(parts[0::2], axis=1))
    h1 = whole(jnp.concatenate(parts[1::2], axis=1))
    ff = w_1.shape[1]
    rows = [whole(v).astype(f32) for v in (fg, fs, os, sg, ss, rs)]
    sm = jnp.concatenate([jnp.stack(rows), jnp.zeros((10, D), f32)], axis=0)
    wide = jnp.tile(whole(es).astype(f32)[None], (8, 1))
    bias = whole(table).astype(f32).reshape(HEADS, BUCKETS)
    bd = bias[:, bucket_of(jnp.arange(256, dtype=jnp.int32))]
    w_1 = whole(w_1)
    out, igrad, d_a, d_o, d_1, d_2, smg, esg, tg = local_layer(
        x,
        documents,
        g,
        h0,
        h1,
        whole(w_o),
        w_1[:, : ff // 2],
        w_1[:, ff // 2 :],
        whole(w_2),
        sm,
        wide,
        bd,
    )
    return (
        out,
        igrad,
        mine(smg[0]),
        mine(smg[1]),
        mine(d_a),
        mine(tg[:, :BUCKETS].reshape(HEADS * BUCKETS)),
        mine(d_o),
        mine(smg[2]),
        mine(smg[3]),
        mine(smg[4]),
        mine(d_1),
        mine(esg[0]),
        mine(d_2),
        mine(smg[5]),
    )


def solution(mesh):
    rows, flat = P(AXES, None), P(AXES)
    dp_size, fsdp_size = mesh.shape["dp"], mesh.shape["fsdp"]
    one_kernel = (dp_size, fsdp_size) == (16, 2)
    return jax.shard_map(
        whole_body(dp_size, fsdp_size) if one_kernel else split_body,
        mesh=mesh,
        in_specs=(
            rows,
            rows,
            flat,
            flat,
            rows,
            flat,
            rows,
            flat,
            flat,
            flat,
            rows,
            flat,
            rows,
            flat,
            rows,
        ),
        out_specs=(rows, rows, flat, flat, rows, flat, rows, flat, flat, flat, rows, flat, rows, flat),
        check_vma=False,
    )
```

```python
import types

import jax
import jax.numpy as jnp
from jax import lax
from jax.experimental import pallas as pl
from jax.experimental.pallas import tpu as pltpu
from jax.sharding import PartitionSpec as P

D = 512
HEADS = 8
HEAD_DIM = 64
BUCKETS = 32
LONGEST = 512
TILE = 128
PAIRS = HEADS // 2
HALF = D // 2
BLOCK = 512
WIDE = 512
NEG = -1e30
eps = 1e-05
far_reach = 128

bf16 = jnp.bfloat16
f32 = jnp.float32
AXES = ("dp", "fsdp")


def iota(shape, dim):
    return lax.broadcasted_iota(jnp.int32, shape, dim)


def bucket_of(distance):
    exact_count = BUCKETS // 2
    counted = jnp.minimum(distance, exact_count)
    for level_j in range(1, exact_count):
        border = int(exact_count * (far_reach / exact_count) ** (level_j / exact_count))
        counted = counted + (distance >= border).astype(jnp.int32)
    return counted


def dot_nn(a, b):
    return lax.dot_general(a, b, (((1,), (0,)), ((), ())), preferred_element_type=f32)


def dot_nt(a, b):
    return lax.dot_general(a, b, (((1,), (1,)), ((), ())), preferred_element_type=f32)


def dot_tn(a, b):
    return lax.dot_general(a, b, (((0,), (0,)), ((), ())), preferred_element_type=f32)


def onehot(mask):
    return jnp.where(mask, 1.0, 0.0).astype(bf16)


def standardize(v):
    center = v - jnp.mean(v, axis=-1, keepdims=True)
    spread = jnp.mean(center * center, axis=-1, keepdims=True)
    rstd = lax.rsqrt(spread + eps)
    return center * rstd, rstd


def standardize_back(dx, xh, rstd):
    return rstd * (
        dx
        - jnp.mean(dx, axis=-1, keepdims=True)
        - xh * jnp.mean(dx * xh, axis=-1, keepdims=True)
    )


def gelu_parts(h):
    phi = 0.5 + 0.5 * lax.erf(h * 0.7071067811865476)
    return h * phi, phi + h * (0.3989422804014327 * jnp.exp(-0.5 * h * h))


def split_heads(t):
    top = iota(t.shape, 0) < HEAD_DIM
    zero = jnp.zeros_like(t)
    return jnp.concatenate([jnp.where(top, t, zero), jnp.where(top, zero, t)], axis=1)


def join_heads(t):
    n = t.shape[1] // 2
    return jnp.concatenate([t[:HEAD_DIM, :n], t[HEAD_DIM:, n:]], axis=0)


def unpack_small(r, n):
    packed = r.WH[0][:, 3 * HALF :]
    rows, lanes = iota((16 * n, D), 0), iota((16 * n, D), 1)
    per = D // n
    rep = onehot(iota((128, D), 1) % per == iota((128, D), 0))
    wide = dot_nn(packed, rep)
    wide = jnp.where(lanes // per == rows // 16, wide, 0.0)
    r.sm[...] = jnp.sum(wide.reshape(n, 16, D), axis=0)
    per = HEADS * BUCKETS // n
    group = BUCKETS // per
    pick = onehot(iota((n, 16 * n), 1) == 16 * iota((n, 16 * n), 0) + 7)
    bucket = bucket_of(iota((128, 256), 1))
    rep = onehot(bucket % per == iota((128, 256), 0))
    wide = dot_nn(dot_nn(pick, packed).astype(bf16), rep)
    bucket = bucket_of(iota((n, 256), 1))
    wide = jnp.where(bucket // per == iota((n, 256), 0) % group, wide, 0.0).astype(bf16)
    gather = onehot(iota((HEADS, n), 1) // group == iota((HEADS, n), 0))
    r.bd[...] = dot_nn(gather, wide)


def unpack_expand_shift(r, n):
    packed = r.WH[0][:, 3 * HALF :]
    ff = r.es.shape[1]
    per = ff // n
    pick = onehot(iota((n, 16 * n), 1) == 16 * iota((n, 16 * n), 0) + 6)
    rep = onehot(iota((128, ff), 1) % per == iota((128, ff), 0))
    wide = dot_nn(dot_nn(pick, packed).astype(bf16), rep)
    wide = jnp.where(iota((n, ff), 1) // per == iota((n, ff), 0), wide, 0.0)
    r.es[...] = jnp.broadcast_to(jnp.sum(wide, axis=0, keepdims=True), r.es.shape)


def pack_small_grads(r, n):
    rows, lanes = iota((16 * n, D), 0), iota((16 * n, D), 1)
    per = D // n
    wide = jnp.broadcast_to(r.smg[...][None], (n, 16, D)).reshape(16 * n, D)
    wide = jnp.where(lanes // per == rows // 16, wide, 0.0).astype(bf16)
    rep = onehot(iota((128, D), 1) % per == iota((128, D), 0))
    packed = dot_nt(wide, rep)
    ff = r.esg.shape[1]
    per = ff // n
    rep = onehot(iota((128, ff), 1) % per == iota((128, ff), 0))
    wide = jnp.broadcast_to(r.esg[0:1, :], (n, ff))
    wide = jnp.where(iota((n, ff), 1) // per == iota((n, ff), 0), wide, 0.0).astype(bf16)
    part = dot_nt(wide, rep).astype(bf16)
    place = onehot(iota((16 * n, n), 0) == 16 * iota((16 * n, n), 1) + 6)
    packed = packed + dot_nn(place, part)
    per = HEADS * BUCKETS // n
    group = BUCKETS // per
    spread = onehot(iota((n, HEADS), 0) // group == iota((n, HEADS), 1))
    wide = dot_nn(spread, r.tg[...].astype(bf16))
    wide = jnp.where(iota((n, 128), 1) // per == iota((n, 128), 0) % group, wide, 0.0)
    rep = onehot(iota((128, 128), 1) % per == iota((128, 128), 0))
    part = dot_nt(wide.astype(bf16), rep).astype(bf16)
    place = onehot(iota((16 * n, n), 0) == 16 * iota((16 * n, n), 1) + 7)
    return packed + dot_nn(place, part)


def over_rows(length, body, block=BLOCK, unroll=2):
    def rows(i, c):
        for u in range(unroll):
            body(pl.ds(pl.multiple_of((i * unroll + u) * block, block), block))
        return c

    lax.fori_loop(0, length // block // unroll, rows, 0)


def standardize_first(r):
    def rows(s):
        r.xh2[s, :] = standardize(r.x[s, :].astype(f32))[0]

    over_rows(r.x.shape[0], rows, 256, 1)


def norm_first(r):
    def rows(s):
        r.na[s, :] = (r.xh2[s, :] * r.sm[0:1, :] + r.sm[1:2, :]).astype(bf16)

    over_rows(r.x.shape[0], rows, 256, 1)


def masks(r):
    length = r.docs.shape[1]
    same = iota((128, length), 0) == r.docs[...]
    r.kd[...] = jnp.where(same, 1.0, 0.0).T.astype(bf16)
    differ = jnp.logical_and(iota((128, length), 0) < 8, jnp.logical_not(same))
    r.qd[...] = jnp.where(differ, NEG, 0.0).astype(bf16)


def near_bias(r):
    for h in range(HEADS):
        by_dist = r.bd[h : h + 1, :]
        by_dist = by_dist - by_dist[:, 255:256]
        line = jnp.concatenate([jnp.full((1, TILE), NEG, f32), by_dist], axis=1)
        line = jnp.broadcast_to(line, (TILE, 3 * TILE))
        line = pltpu.roll(line, 0, 1, stride=1, stride_axis=0)
        half = slice((h % 2) * TILE, (h % 2 + 1) * TILE)
        r.near[h // 2, 0:TILE, half] = line[:, 2 * TILE :]
        r.near[h // 2, TILE:, half] = line[:, TILE : 2 * TILE]


def project(r, half):
    def rows(s):
        out = dot_nn(r.na[s, :], r.WH[half][:, 0 : 3 * HALF])
        q = (out[:, :HALF].astype(bf16) * bf16(HEAD_DIM**-0.5)).T
        k = out[:, HALF : 2 * HALF].astype(bf16)
        v = out[:, 2 * HALF :].astype(bf16)
        for j in range(2):
            lanes = slice(j * 128, (j + 1) * 128)
            r.qt[2 * half + j, :, s] = q[lanes, :]
            r.k[2 * half + j, s, :] = k[:, lanes]
            r.v[2 * half + j, s, :] = v[:, lanes]

    over_rows(r.x.shape[0], rows)


def bands(length):
    first = 0
    for b in range(length // TILE):
        low = max(0, b - LONGEST // TILE)
        count = (b + 1 - low) * TILE
        yield b, slice(low * TILE, (b + 1) * TILE), slice(b * TILE, (b + 1) * TILE), first, count
        first += count


def band_rows(length):
    return sum(count for _, _, _, _, count in bands(length))


def attend_forward(r, p):
    near = r.near[p]
    lanes = pl.ds(pl.multiple_of(p * 128, 128), 128)
    plan = list(bands(r.x.shape[0]))

    def scores(b, ks, qs, first, count):
        qd = r.qd[:, qs]
        rhs = jnp.concatenate(
            [split_heads(r.qt[p, :, qs]), jnp.concatenate([qd, qd], axis=1)], axis=0
        )
        lhs = jnp.concatenate([r.k[p, ks, :], r.kd[ks, :]], axis=1)
        st = dot_nn(lhs, rhs)
        if count > 2 * TILE:
            return jnp.concatenate([st[: count - 2 * TILE], st[count - 2 * TILE :] + near], axis=0)
        return st + near[2 * TILE - count :]

    def soften(st, b, first, count):
        lifted = jnp.exp(st - jnp.max(st, axis=0, keepdims=True))
        inverse = 1.0 / jnp.sum(lifted, axis=0, keepdims=True)
        weights = lifted.astype(bf16)
        r.P[p, first : first + count, :] = weights
        r.inv[p, b : b + 1, :] = inverse
        return weights, inverse

    def attended(weights, inverse, ks, qs):
        ot = join_heads(dot_tn(r.v[p, ks, :], weights) * inverse)
        r.ot[p, :, qs] = ot
        r.att[qs, lanes] = ot.T.astype(bf16)

    AHEAD = 1
    queue, soft = [], []
    steps = len(plan)
    for i in range(steps + 2):
        if i < steps:
            queue.append(scores(*plan[i]))
        if 1 <= i <= steps:
            b, ks, qs, first, count = plan[i - 1]
            soft.append(soften(queue.pop(0), b, first, count))
        if 2 <= i:
            b, ks, qs, first, count = plan[i - 2]
            attended(*soft.pop(0), ks, qs)


def attend_backward(r, p):
    length = r.x.shape[0]
    r.dk[...] = jnp.zeros_like(r.dk)
    r.dv[...] = jnp.zeros_like(r.dv)
    r.acc[...] = jnp.zeros_like(r.acc)
    inner = pl.multiple_of((p // 2) * 3 * HALF + (p % 2) * 128, 128)
    top = iota((128, TILE), 0) < HEAD_DIM
    plan = list(bands(length))

    def soft_grad(b, ks, qs, first, count):
        inverse = r.inv[p, b : b + 1, :]
        scale = jnp.where(top, inverse[:, :TILE], inverse[:, TILE:])
        dot_ = (r.dot[p, :, qs].astype(f32) * scale).astype(bf16)
        prod = dot_.astype(f32) * r.ot[p, :, qs]
        delta = jnp.concatenate(
            [
                jnp.sum(prod[:HEAD_DIM], axis=0, keepdims=True),
                jnp.sum(prod[HEAD_DIM:], axis=0, keepdims=True),
            ],
            axis=1,
        )
        dcat = split_heads(dot_)
        return dcat, delta, dot_nn(r.v[p, ks, :], dcat)

    def score_grad(dcat, delta, dpt, first, count):
        weights = r.P[p, first : first + count, :]
        ds = weights.astype(f32) * (dpt - delta)
        if count >= 2 * TILE:
            r.acc[...] += ds[count - 2 * TILE :]
        else:
            r.acc[TILE:, :] += ds
        return weights, dcat, ds.astype(bf16)

    def operand_grads(weights, dcat, dsb, ks, qs):
        r.dv[ks, :] += dot_nt(weights, dcat)
        r.dk[ks, :] += dot_nt(dsb, split_heads(r.qt[p, :, qs]))
        dqt = join_heads(dot_tn(r.k[p, ks, :], dsb)) * HEAD_DIM**-0.5
        r.gh[qs, pl.ds(inner, 128)] = dqt.T.astype(bf16)

    soft, score = [], []
    steps = len(plan)
    for i in range(steps + 2):
        if i < steps:
            soft.append(soft_grad(*plan[i]))
        if 1 <= i <= steps:
            b, ks, qs, first, count = plan[i - 1]
            score.append(score_grad(*soft.pop(0), first, count))
        if 2 <= i:
            b, ks, qs, first, count = plan[i - 2]
            operand_grads(*score.pop(0), ks, qs)
    r.gh[:, pl.ds(HALF + inner, 128)] = r.dk[...].astype(bf16)
    r.gh[:, pl.ds(2 * HALF + inner, 128)] = r.dv[...].astype(bf16)
    zero = jnp.zeros((TILE, TILE), f32)
    rows = iota((TILE, 3 * TILE), 0)
    for h in range(2):
        half = slice(h * TILE, (h + 1) * TILE)
        line = jnp.concatenate([zero, r.acc[TILE:, half], r.acc[:TILE, half]], axis=1)
        for bit in range(7):
            rolled = pltpu.roll(line, 3 * TILE - (1 << bit), 1)
            line = jnp.where((rows >> bit) & 1 == 1, rolled, line)
        r.lines[pl.ds(2 * p + h, 1), :] = jnp.sum(line, axis=0, keepdims=True)


def table_grad(r):
    by_dist = r.lines[:, TILE:]
    dist = iota((2 * TILE, 128), 0)
    near = jnp.logical_and(bucket_of(dist) == iota((2 * TILE, 128), 1), dist < 2 * TILE)
    near = jnp.logical_and(near, iota((2 * TILE, 128), 1) < BUCKETS - 1)
    counted = lax.dot_general(
        by_dist,
        jnp.where(near, 1.0, 0.0),
        (((1,), (0,)), ((), ())),
        precision=lax.Precision.HIGHEST,
        preferred_element_type=f32,
    )
    rest = -jnp.sum(counted, axis=1, keepdims=True)
    r.tg[...] = jnp.where(iota((HEADS, 128), 1) == BUCKETS - 1, rest, counted)


def before_ff(r):
    r.smg[...] = jnp.zeros_like(r.smg)
    r.esg[...] = jnp.zeros_like(r.esg)

    def rows(s):
        residual = r.x[s, :].astype(f32) + dot_nn(r.att[s, :], r.WO[...]) + r.sm[2:3, :]
        xh, rstd = standardize(residual)
        r.xh2[s, :] = xh
        r.rstd2[s, :] = rstd
        r.nf[s, :] = (xh * r.sm[3:4, :] + r.sm[4:5, :]).astype(bf16)
        r.branch[s, :] = residual + r.sm[5:6, :]

    over_rows(r.x.shape[0], rows)


def feed_forward(r, f):
    cols = slice(f * WIDE, (f + 1) * WIDE)
    half = r.W1[f // 2]
    inner = slice((f % 2) * WIDE, (f % 2 + 1) * WIDE)

    def rows(s):
        hidden = dot_nn(r.nf[s, :], half[:, inner]) + r.es[0:1, cols]
        active, slope = gelu_parts(hidden)
        r.act[s, cols] = active.astype(bf16)
        r.gh[s, cols] = slope.astype(bf16)

    over_rows(r.x.shape[0], rows, 256, 4)


def feed_backward(r, f):
    cols = slice(f * WIDE, (f + 1) * WIDE)

    def rows(s):
        gh = dot_nt(r.g[s, :], r.W2[cols, :]) * r.gh[s, cols].astype(f32)
        r.esg[0:1, cols] += jnp.sum(gh, axis=0, keepdims=True)
        r.gh[s, cols] = gh.astype(bf16)

    over_rows(r.x.shape[0], rows)


def after_ff(r, s):
    ff = r.es.shape[1]
    gnf = dot_nt(r.gh[s, : ff // 2], r.W1[0][...]) + dot_nt(r.gh[s, ff // 2 :], r.W1[1][...])
    xh = r.xh2[s, :]
    gf = r.g[s, :].astype(f32)
    grad = gf + standardize_back(gnf * r.sm[3:4, :], xh, r.rstd2[s, :])
    r.xh2[s, :] = grad
    gb = grad.astype(bf16)
    r.gb[s, :] = gb
    r.smg[2:3, :] += jnp.sum(gb.astype(f32), axis=0, keepdims=True)
    r.smg[3:4, :] += jnp.sum(gnf * xh, axis=0, keepdims=True)
    r.smg[4:5, :] += jnp.sum(gnf, axis=0, keepdims=True)
    r.smg[5:6, :] += jnp.sum(gf, axis=0, keepdims=True)
    dot_ = dot_nt(gb, r.WO[...]).astype(bf16).T
    for p in range(PAIRS):
        r.dot[p, :, s] = dot_[p * 128 : (p + 1) * 128, :]


def output(r, s):
    r.nf[s, :] = (r.branch[s, :] + dot_nn(r.act[s, :], r.W2[...])).astype(bf16)


def half_columns(half):
    return slice(half * 3 * HALF, (half + 1) * 3 * HALF)


def pair_columns(ref, rows, p, base=0):
    at = base + (p % 2) * 128
    return jnp.concatenate(
        [ref[rows, part * HALF + at : part * HALF + at + 128] for part in range(3)], axis=1
    )


def back_project(r, half, pair=None):
    def rows(s):
        if pair is None:
            grads, weight = r.gh[s, half_columns(half)], r.WH[half][:, 0 : 3 * HALF]
        else:
            grads = pair_columns(r.gh, s, pair, half * 3 * HALF)
            weight = pair_columns(r.WH[half], slice(None), pair)
        part = dot_nt(grads, weight)
        r.gnf[s, :] = part if half == 0 else r.gnf[s, :] + part

    over_rows(r.x.shape[0], rows)


def last(r):
    def rows(s):
        gna = r.gnf[s, :]
        xh, rstd = standardize(r.x[s, :].astype(f32))
        r.xh2[s, :] += standardize_back(gna * r.sm[0:1, :], xh, rstd)
        r.smg[0:1, :] += jnp.sum(gna * xh, axis=0, keepdims=True)
        r.smg[1:2, :] += jnp.sum(gna, axis=0, keepdims=True)

    over_rows(r.x.shape[0], rows)


def weight_grad(left, right, step, put):
    count = left.shape[1] // step
    if count == 1:
        put(0, dot_tn(left[...], right()))
        return

    def rows(i, c):
        put(i, dot_tn(left[:, pl.ds(pl.multiple_of(i * step, step), step)], right()))
        return c

    lax.fori_loop(0, count, rows, 0)


class Place:
    def __init__(self, dp_size, fsdp_size):
        dp, x = lax.axis_index("dp"), lax.axis_index("fsdp")
        self.z, self.y, self.c, self.x = dp // 4, (dp // 2) % 2, dp % 2, x
        self.zs = dp_size // 4

    def zpeer(self, m):
        z = self.z
        return (z, z + 1 - 2 * (z % 2), (z + 2) % 4, 3 - z)[m]

    def index(self, m, t, other=False):
        x = 1 - self.x if t in (1, 3) else self.x
        y = 1 - self.y if t in (2, 3) else self.y
        c = 1 - self.c if other else self.c
        return ((self.zpeer(m) * 2 + y) * 2 + c) * 2 + x

    def inner(self, t, other=False):
        x = 1 - self.x if t in (1, 3) else self.x
        y = 1 - self.y if t in (2, 3) else self.y
        c = 1 - self.c if other else self.c
        return (y * 2 + c) * 2 + x

    def device(self, m=0, t=0, other=False):
        x = 1 - self.x if t in (1, 3) else self.x
        y = 1 - self.y if t in (2, 3) else self.y
        c = 1 - self.c if other else self.c
        return ((self.zpeer(m) * 2 + y) * 2 + c, x)

    def neighbours(self):
        return [self.device(m=m) for m in (1, 2, 3)] + [
            self.device(t=1),
            self.device(t=2),
            self.device(t=3),
            self.device(other=True),
        ]


def greet(place):
    barrier = pltpu.get_barrier_semaphore()
    for peer in place.neighbours():
        pl.semaphore_signal(
            barrier, inc=1, device_id=peer, device_id_type=pl.DeviceIdType.MESH
        )


def enter():
    pl.semaphore_wait(pltpu.get_barrier_semaphore(), 7)


GATHER_SEMS, SCATTER_SEMS = 8, 9
X, Y, OPPOSITE_A, OPPOSITE_B, SIBLING = 3, 4, 5, 6, 7


class Gather:
    def __init__(self, place, whole, rho, half, send, recv):
        self.place, self.whole, self.rho, self.half = place, whole, rho, half
        self.send, self.recv = send, recv

    def view(self, shard, part=None, count=1):
        rows = pl.ds(pl.multiple_of(shard * self.rho, 16), count * self.rho)
        if part is None:
            return self.whole.at[rows, :]
        cols = slice(0, self.half) if part == 0 else slice(self.half, self.whole.shape[1])
        return self.whole.at[rows, cols]

    def copy(self, ref, sem, device):
        return pltpu.make_async_remote_copy(
            src_ref=ref,
            dst_ref=ref,
            send_sem=self.send,
            recv_sem=self.recv.at[sem],
            device_id=device,
            device_id_type=pl.DeviceIdType.MESH,
        )

    def start(self, shard, sem, device, part=None):
        self.copy(self.view(shard, part), sem, device).start()

    def arrive(self, count, sem, part=None):
        ref = self.view(0, part, count)
        self.copy(ref, sem, self.place.device(other=True)).wait_recv()

    def along_z(self):
        at = self.place
        for m in (1, 2, 3):
            self.start(at.index(0, 0), m - 1, at.device(m=m))

    def first(self):
        self.along_z()
        self.spread(0)

    def spread(self, m):
        at = self.place
        shard = at.index(m, 0)
        self.start(shard, X, at.device(t=1))
        self.start(shard, Y, at.device(t=2))
        if self.half is None:
            self.start(shard, OPPOSITE_A, at.device(t=3))
        self.start(shard, SIBLING, at.device(other=True))

    def second(self):
        for m in (1, 2, 3):
            self.arrive(1, m - 1)
            self.spread(m)

    def third(self):
        at = self.place
        self.arrive(4, X)
        for m in range(4):
            if self.half is not None:
                self.start(at.index(m, 1), OPPOSITE_A, at.device(t=2), 0)
        for m in range(4):
            self.start(at.index(m, 1), SIBLING, at.device(other=True))
        self.arrive(4, Y)
        for m in range(4):
            if self.half is not None:
                self.start(at.index(m, 2), OPPOSITE_B, at.device(t=1), 1)
        for m in range(4):
            self.start(at.index(m, 2), SIBLING, at.device(other=True))

    def fourth(self):
        at = self.place
        if self.half is None:
            self.arrive(4, OPPOSITE_A)
        else:
            self.arrive(4, OPPOSITE_A, 0)
            self.arrive(4, OPPOSITE_B, 1)
        for m in range(4):
            self.start(at.index(m, 3), SIBLING, at.device(other=True))

    def finish(self):
        self.arrive(16, SIBLING)

    def drain(self):
        self.copy(self.view(0, None, 31), X, self.place.device(other=True)).wait_send()


class Scatter:
    def __init__(self, place, full, bufs, half, send, recv, emit):
        self.place, self.full, self.half, self.emit = place, full, half, emit
        self.sib, self.ra, self.rb, self.rx, self.ry, self.rz = bufs
        self.send, self.recv = send, recv

    def copy(self, src, dst, sem, device):
        group = 0 if sem < 4 else 1 if sem < 8 else 2
        return pltpu.make_async_remote_copy(
            src_ref=src,
            dst_ref=dst,
            send_sem=self.send.at[group],
            recv_sem=self.recv.at[sem],
            device_id=device,
            device_id_type=pl.DeviceIdType.MESH,
        )

    def start(self, src, dst, sem, device):
        self.copy(src, dst, sem, device).start()

    def arrive(self, dst, sem):
        self.copy(dst, dst, sem, self.place.device(other=True)).wait_recv()

    def first(self):
        at = self.place
        for t in (3, 1, 2, 0):
            self.start(
                self.full.at[:, at.inner(t, other=True)], self.sib.at[t], t, at.device(other=True)
            )

    def merge(self, t):
        self.arrive(self.sib.at[t], t)
        self.sib[t] += self.full[:, self.place.inner(t)]

    def second(self):
        at = self.place
        self.merge(3)
        if self.half is None:
            self.start(self.sib.at[3], self.ra, 4, at.device(t=3))
            self.merge(1)
            self.start(self.sib.at[1], self.rx, 6, at.device(t=1))
            self.merge(2)
            self.start(self.sib.at[2], self.ry, 7, at.device(t=2))
        else:
            self.start(self.sib.at[3, :, :, : self.half], self.ra, 4, at.device(t=1))
            self.start(self.sib.at[3, :, :, self.half :], self.rb, 5, at.device(t=2))

    def third(self):
        at = self.place
        if self.half is None:
            return
        self.merge(1)
        self.merge(2)
        self.arrive(self.rb, 5)
        self.sib[1, :, :, self.half :] += self.rb[...]
        self.start(self.sib.at[1], self.rx, 6, at.device(t=1))
        self.arrive(self.ra, 4)
        self.sib[2, :, :, : self.half] += self.ra[...]
        self.start(self.sib.at[2], self.ry, 7, at.device(t=2))

    def fourth(self):
        at = self.place
        self.merge(0)
        self.arrive(self.rx, 6)
        self.arrive(self.ry, 7)
        total = self.rx[...].astype(f32) + self.ry[...].astype(f32)
        if self.half is None:
            self.arrive(self.ra, 4)
            total = total + self.ra[...].astype(f32)
        self.sib[0] += total.astype(bf16)
        for m in (1, 2, 3):
            self.start(self.sib.at[0, at.zpeer(m)], self.rz.at[m - 1], 8, at.device(m=m))

    def fifth(self):
        self.arrive(self.rz, 8)
        total = self.sib[0, self.place.z].astype(f32)
        for m in (1, 2, 3):
            total = total + self.rz[m - 1].astype(f32)
        self.emit(total)

    def drain(self):
        for sem, ref in ((0, self.sib), (4, self.sib.at[0:3]), (8, self.rz)):
            self.copy(ref, ref, sem, self.place.device(other=True)).wait_send()


class ScatterByPlane(Scatter):
    def copy(self, src, dst, sem, device):
        group = 0 if sem < 16 else 1 if sem < 32 else 2
        return pltpu.make_async_remote_copy(
            src_ref=src,
            dst_ref=dst,
            send_sem=self.send.at[group],
            recv_sem=self.recv.at[sem],
            device_id=device,
            device_id_type=pl.DeviceIdType.MESH,
        )

    def first(self, z):
        at = self.place
        for t in (3, 1, 2, 0):
            self.start(
                self.full.at[z, at.inner(t, other=True)],
                self.sib.at[t, z],
                4 * t + z,
                at.device(other=True),
            )

    def merge(self, t, z):
        self.arrive(self.sib.at[t, z], 4 * t + z)
        self.sib[t, z] += self.full[z, self.place.inner(t)]

    def second(self, z):
        at = self.place
        self.merge(3, z)
        self.start(self.sib.at[3, z, :, : self.half], self.ra.at[z], 16 + z, at.device(t=1))
        self.start(self.sib.at[3, z, :, self.half :], self.rb.at[z], 20 + z, at.device(t=2))

    def third(self, z):
        at = self.place
        self.merge(1, z)
        self.merge(2, z)
        self.arrive(self.rb.at[z], 20 + z)
        self.sib[1, z, :, self.half :] += self.rb[z]
        self.start(self.sib.at[1, z], self.rx.at[z], 24 + z, at.device(t=1))
        self.arrive(self.ra.at[z], 16 + z)
        self.sib[2, z, :, : self.half] += self.ra[z]
        self.start(self.sib.at[2, z], self.ry.at[z], 28 + z, at.device(t=2))

    def fourth(self):
        at = self.place
        for z in range(4):
            self.merge(0, z)
            self.arrive(self.rx.at[z], 24 + z)
            self.arrive(self.ry.at[z], 28 + z)
            total = self.rx[z].astype(f32) + self.ry[z].astype(f32)
            self.sib[0, z] += total.astype(bf16)
        for m in (1, 2, 3):
            self.start(self.sib.at[0, at.zpeer(m)], self.rz.at[m - 1], 32, at.device(m=m))

    def fifth(self):
        self.arrive(self.rz, 32)
        total = self.sib[0, self.place.z].astype(f32)
        for m in (1, 2, 3):
            total = total + self.rz[m - 1].astype(f32)
        self.emit(total)

    def drain(self):
        for sem, ref in ((0, self.sib), (16, self.sib.at[0:3]), (32, self.rz)):
            self.copy(ref, ref, sem, self.place.device(other=True)).wait_send()


def scatter_bufs(rho, cols, half):
    first = cols if half is None else half
    rest = 128 if half is None else cols - half
    return [
        pltpu.VMEM((4, 4, rho, cols), bf16),
        pltpu.VMEM((4, rho, first), bf16),
        pltpu.VMEM((4, rho, rest), bf16),
        pltpu.VMEM((4, rho, cols), bf16),
        pltpu.VMEM((4, rho, cols), bf16),
        pltpu.VMEM((3, rho, cols), bf16),
    ]


def over_pairs(attend, r, first, end, pump):
    def one(p, c):
        attend(r, p)
        for pair in range(first, end):
            if pair in pump:

                @pl.when(p == pair)
                def _():
                    pump[pair]()
        return c

    lax.fori_loop(first, end, one, 0)


def work_scratch(length, ff):
    tokens = band_rows(length)
    return dict(
        x=pltpu.VMEM((length, D), bf16),
        na=pltpu.VMEM((length, D), bf16),
        kd=pltpu.VMEM((length, 128), bf16),
        qd=pltpu.VMEM((128, length), bf16),
        near=pltpu.VMEM((PAIRS, 2 * TILE, 2 * TILE), f32),
        qt=pltpu.VMEM((PAIRS, 128, length), bf16),
        k=pltpu.VMEM((PAIRS, length, 128), bf16),
        v=pltpu.VMEM((PAIRS, length, 128), bf16),
        P=pltpu.VMEM((PAIRS, tokens, 2 * TILE), bf16),
        inv=pltpu.VMEM((PAIRS, length // TILE, 2 * TILE), f32),
        ot=pltpu.VMEM((PAIRS, 128, length), f32),
        att=pltpu.VMEM((length, D), bf16),
        xh2=pltpu.VMEM((length, D), f32),
        rstd2=pltpu.VMEM((length, 1), f32),
        branch=pltpu.VMEM((length, D), f32),
        gnf=pltpu.VMEM((length, D), f32),
        nf=pltpu.VMEM((length, D), bf16),
        act=pltpu.VMEM((length, ff), bf16),
        gh=pltpu.VMEM((length, ff), bf16),
        gb=pltpu.VMEM((length, D), bf16),
        dot=pltpu.VMEM((PAIRS, 128, length), bf16),
        dk=pltpu.VMEM((length, 128), f32),
        dv=pltpu.VMEM((length, 128), f32),
        acc=pltpu.VMEM((2 * TILE, 2 * TILE), f32),
        lines=pltpu.VMEM((HEADS, 3 * TILE), f32),
    )


def small_scratch(ff):
    return dict(
        sm=pltpu.VMEM((16, D), f32),
        es=pltpu.VMEM((8, ff), f32),
        bd=pltpu.VMEM((HEADS, 256), f32),
        smg=pltpu.VMEM((16, D), f32),
        esg=pltpu.VMEM((8, ff), f32),
        tg=pltpu.VMEM((HEADS, 128), f32),
    )


def run_kernel(kernel, operands, out_shape, scratch, in_hbm=(), out_hbm=(), **params):
    names = list(scratch)
    count = len(operands) + len(out_shape)

    def named(*refs):
        kernel(refs[: len(operands)], refs[len(operands) : count], dict(zip(names, refs[count:])))

    def specs(number, hbm):
        return [
            pl.BlockSpec(memory_space=pl.ANY if i in hbm else pltpu.VMEM) for i in range(number)
        ]

    return pl.pallas_call(
        named,
        out_shape=out_shape,
        in_specs=specs(len(operands), in_hbm),
        out_specs=specs(len(out_shape), out_hbm),
        scratch_shapes=[scratch[name] for name in names],
        compiler_params=pltpu.CompilerParams(vmem_limit_bytes=VMEM_BYTES, **params),
    )(*operands)


VMEM_BYTES = 63 * 1024 * 1024


def whole_layer(x, documents, g, small, w_a, w_o, w_1, w_2, dp_size, fsdp_size):
    n = dp_size * fsdp_size
    length, ff = x.shape[0], w_1.shape[1]
    ra, r2 = w_1.shape[0], w_2.shape[0]
    gathered = dict(
        H0=(ra, 3 * HALF + 128, None),
        H1=(ra, 3 * HALF, None),
        WO=(ra, D, HALF),
        W2=(r2, D, HALF),
        W1a=(ra, ff // 2, ff // 4),
        W1b=(ra, ff // 2, ff // 4),
    )
    scattered = dict(
        d1a=(ra, ff // 2, ff // 4),
        d1b=(ra, ff // 2, ff // 4),
        d2=(r2, D, HALF),
        dO=(ra, D, HALF),
        dH=(ra, 3 * HALF, HALF),
        dT2=(ra, 384, None),
        dT3=(ra, 384, None),
        dS=(ra, 128, None),
    )
    scratch = dict(work_scratch(length, ff), **small_scratch(ff))
    scratch["g"] = pltpu.VMEM((length, D), bf16)
    for name, (rho, cols, _) in gathered.items():
        scratch[name] = pltpu.VMEM((n * rho, cols), bf16)
    for name, (rho, cols, half) in scattered.items():
        scratch[name] = pltpu.VMEM((4, 8, rho, cols), bf16)
        for j, buf in enumerate(scatter_bufs(rho, cols, half)):
            scratch["%s_%d" % (name, j)] = buf
    dma = pltpu.SemaphoreType.DMA
    scratch.update(
        gsend=dma((len(gathered),)),
        grecv=dma((len(gathered), GATHER_SEMS)),
        prec=dma((33,)),
        ssend=dma((len(scattered), 3)),
        srecv=dma((len(scattered), SCATTER_SEMS)),
        move=dma((4,)),
    )

    def kernel(ins, outs, s):
        r = types.SimpleNamespace(**s)
        x_in, r.docs, g_in = ins[:3]
        vectors, (own_a, own_o, own_1, own_2) = ins[3:11], ins[11:]
        out, igrad, out_a, out_o, out_1, out_2, out_s = outs
        r.WH, r.W1 = [r.H0, r.H1], [r.W1a, r.W1b]
        at = Place(dp_size, fsdp_size)
        get_x = pltpu.make_async_copy(x_in, r.x, r.move.at[0])
        get_g = pltpu.make_async_copy(g_in, r.g, r.move.at[1])
        put_out = pltpu.make_async_copy(r.nf, out, r.move.at[2])
        put_igrad = pltpu.make_async_copy(r.xh2, igrad, r.move.at[3])
        get_x.start()
        get_g.start()
        greet(at)
        mine = at.index(0, 0)
        rows_a = pl.ds(pl.multiple_of(mine * ra, 16), ra)
        rows_2 = pl.ds(pl.multiple_of(mine * r2, 16), r2)
        for half, ref in enumerate(r.WH):
            for part in range(3):
                ref[rows_a, part * HALF : (part + 1) * HALF] = own_a[
                    :, part * D + half * HALF : part * D + (half + 1) * HALF
                ]
        lines = [
            jnp.concatenate(
                [v[...].astype(f32), jnp.zeros((1, 128 - v.shape[1]), f32)], axis=1
            )
            for v in vectors
        ]
        lines.append(jnp.zeros((ra - len(lines), 128), f32))
        r.H0[rows_a, 3 * HALF :] = jnp.concatenate(lines, axis=0).astype(bf16)
        r.WO[rows_a, :] = own_o[...]
        r.W2[rows_2, :] = own_2[...]
        for half, ref in enumerate(r.W1):
            ref[rows_a, :] = own_1[:, half * ff // 2 : (half + 1) * ff // 2]
        gathers = {
            name: Gather(at, s[name], rho, half, r.gsend.at[i], r.grecv.at[i])
            for i, (name, (rho, _, half)) in enumerate(gathered.items())
        }
        h0, h1, wo, w2, w1a, w1b = gathers.values()
        enter()
        h0.first()
        masks(r)
        get_x.wait()
        standardize_first(r)
        h0.second()
        h1.first()
        wo.first()
        h0.third()
        h0.fourth()
        h0.finish()
        unpack_small(r, n)
        norm_first(r)
        h1.second()
        w1a.first()
        near_bias(r)
        wo.second()
        project(r, 0)
        w1b.first()
        h1.third()
        w1a.second()

        def pump_0():
            h1.fourth()
            wo.third()
            w2.first()

        def pump_1():
            w1a.third()
            w1b.second()
            h1.finish()

        def pump_2():
            wo.fourth()
            w2.second()

        def pump_3():
            w1a.fourth()
            w1b.third()
            wo.finish()

        over_pairs(attend_forward, r, 0, 2, {0: pump_0, 1: pump_1})
        project(r, 1)
        over_pairs(attend_forward, r, 2, 4, {2: pump_2, 3: pump_3})
        unpack_expand_shift(r, n)
        before_ff(r)
        w1a.finish()
        get_g.wait()

        def emit_into(ref, cols):
            def emit(total):
                ref[:, cols] = total

            return emit

        def emit_pairs(pairs):
            def emit(total):
                wide = 128 * len(pairs)
                for part in range(3):
                    first = part * D + pairs[0] * 128
                    out_a[:, first : first + wide] = total[:, part * wide : (part + 1) * wide]

            return emit

        emits = dict(
            d1a=emit_into(out_1, slice(0, ff // 2)),
            d1b=emit_into(out_1, slice(ff // 2, ff)),
            d2=emit_into(out_2, slice(None)),
            dO=emit_into(out_o, slice(None)),
            dH=emit_pairs((0, 1)),
            dT2=emit_pairs((2,)),
            dT3=emit_pairs((3,)),
            dS=emit_into(out_s, slice(None)),
        )
        scatters = {
            name: (ScatterByPlane if name == "d2" else Scatter)(
                at,
                s[name],
                [s["%s_%d" % (name, j)] for j in range(6)],
                half,
                r.ssend.at[i],
                r.prec if name == "d2" else r.srecv.at[i],
                emits[name],
            )
            for i, (name, (_, _, half)) in enumerate(scattered.items())
        }
        s1a, s1b, s2, so, sh, st2, st3, ss = scatters.values()

        def put_shards(ref, step, rho, first=0):
            count = step // (8 * rho)

            def put(i, value):
                value = value.astype(bf16).reshape(count, 8, rho, value.shape[1])
                ref[pl.ds(count * i, count), :, :, first : first + value.shape[3]] = value

            return put

        def expand_grad(f, ref):
            cols = slice(f * WIDE, (f + 1) * WIDE)
            weight_grad(
                r.nf, lambda: r.gh[:, cols], D, put_shards(ref, D, ra, (f % 2) * WIDE)
            )

        def reduce_grad(f):
            act = r.act[:, f * WIDE : (f + 1) * WIDE]
            r.d2[f] = dot_tn(act, r.g[...]).astype(bf16).reshape(8, r2, D)
            s2.first(f)

        feed_forward(r, 0)
        reduce_grad(0)
        w1b.fourth()
        feed_forward(r, 1)
        reduce_grad(1)
        s2.second(0)
        w1b.finish()
        w2.third()
        feed_forward(r, 2)
        reduce_grad(2)
        s2.second(1)
        feed_forward(r, 3)
        reduce_grad(3)
        s2.third(0)
        s2.second(2)
        w2.fourth()
        s2.third(1)
        w2.finish()
        feed_backward(r, 0)
        expand_grad(0, r.d1a)
        s2.second(3)
        feed_backward(r, 1)
        expand_grad(1, r.d1a)
        s1a.first()
        s2.third(2)
        feed_backward(r, 2)
        expand_grad(2, r.d1b)
        s2.third(3)
        feed_backward(r, 3)
        expand_grad(3, r.d1b)
        s1b.first()
        s1a.second()
        after_ff(r, slice(0, BLOCK))
        s2.fourth()
        for i in range(1, length // BLOCK):
            after_ff(r, slice(i * BLOCK, (i + 1) * BLOCK))
        s1b.second()
        s1a.third()
        weight_grad(r.att, lambda: r.gb[...], D, put_shards(r.dO, D, ra))
        so.first()

        def pump_0():
            so.second()
            s1b.third()

        def pump_1():
            s2.fifth()
            s1a.fourth()
            so.third()

        def pump_2():
            sh.second()
            s1b.fourth()
            so.fourth()

        def pump_3():
            st2.second()
            sh.third()
            s1a.fifth()

        pump = {0: pump_0, 1: pump_1, 2: pump_2, 3: pump_3}
        over_pairs(attend_backward, r, 0, 2, pump)
        weight_grad(
            r.na, lambda: r.gh[:, half_columns(0)], D, put_shards(r.dH, D, ra)
        )
        sh.first()
        back_project(r, 0)
        over_pairs(attend_backward, r, 2, 3, pump)
        weight_grad(
            r.na, lambda: pair_columns(r.gh, slice(None), 2, 3 * HALF), D, put_shards(r.dT2, D, ra)
        )
        st2.first()
        back_project(r, 1, 2)
        over_pairs(attend_backward, r, 3, 4, pump)
        weight_grad(
            r.na, lambda: pair_columns(r.gh, slice(None), 3, 3 * HALF), D, put_shards(r.dT3, D, ra)
        )
        st3.first()
        back_project(r, 1, 3)
        last(r)
        put_igrad.start()
        st3.second()
        table_grad(r)
        r.dS[...] = pack_small_grads(r, n).astype(bf16).reshape(4, 8, ra, 128)
        ss.first()
        output(r, slice(0, BLOCK))
        ss.second()
        sh.fourth()
        st2.fourth()
        for i in range(1, length // BLOCK):
            output(r, slice(i * BLOCK, (i + 1) * BLOCK))
        put_out.start()
        s1b.fifth()
        so.fifth()
        st3.fourth()
        ss.fourth()
        sh.fifth()
        st2.fifth()
        st3.fifth()
        ss.fifth()
        for item in list(gathers.values()) + list(scatters.values()):
            item.drain()
        put_out.wait()
        put_igrad.wait()

    out_shape = [
        jax.ShapeDtypeStruct((length, D), bf16),
        jax.ShapeDtypeStruct((length, D), f32),
        jax.ShapeDtypeStruct((ra, 3 * D), f32),
        jax.ShapeDtypeStruct((ra, D), f32),
        jax.ShapeDtypeStruct((ra, ff), f32),
        jax.ShapeDtypeStruct((r2, D), f32),
        jax.ShapeDtypeStruct((ra, 128), f32),
    ]
    operands = [x, documents, g, *small, w_a, w_o, w_1, w_2]
    return run_kernel(
        kernel,
        operands,
        out_shape,
        scratch,
        in_hbm=(0, 2),
        out_hbm=(0, 1),
        collective_id=0,
        has_side_effects=True,
    )


def hand_out(results, sizes):
    length = results[0].shape[0]
    pieces = 4
    chunk = length // pieces

    def kernel(ins, outs, s):
        buffers = (s["a"], s["b"])

        def move(i, j, back):
            rows = slice(j * chunk, (j + 1) * chunk)
            here = buffers[i].at[rows, :]
            there = (outs if back else ins)[i].at[rows, :]
            sem = s["move"].at[pieces * i + j, int(back)]
            if back:
                return pltpu.make_async_copy(here, there, sem)
            return pltpu.make_async_copy(there, here, sem)

        parts = [(i, j) for j in range(pieces) for i in range(2)]
        for i, j in parts:
            move(i, j, False).start()
        for i in range(2, 6):
            outs[i][...] = ins[i][...]
        for i, size in enumerate(sizes):
            outs[6 + i][...] = ins[6][i : i + 1, :size]
        for i, j in parts:
            move(i, j, False).wait()
            move(i, j, True).start()
        for i, j in parts:
            move(i, j, True).wait()

    out_shape = [jax.ShapeDtypeStruct(v.shape, v.dtype) for v in results[:6]]
    out_shape += [jax.ShapeDtypeStruct((1, size), f32) for size in sizes]
    scratch = dict(
        a=pltpu.VMEM(results[0].shape, results[0].dtype),
        b=pltpu.VMEM(results[1].shape, results[1].dtype),
        move=pltpu.SemaphoreType.DMA((2 * pieces, 2)),
    )
    return run_kernel(
        kernel, list(results), out_shape, scratch, in_hbm=(0, 1), out_hbm=(0, 1)
    )


def local_layer(x, documents, g, h0, h1, w_o, w_1a, w_1b, w_2, sm, es, bd):
    length, ff = x.shape[0], 2 * w_1a.shape[1]
    scratch = dict(work_scratch(length, ff))

    def kernel(ins, outs, s):
        r = types.SimpleNamespace(**s)
        x_in, r.docs, r.g, h0_, h1_, r.WO, w1a_, w1b_, r.W2, r.sm, r.es, r.bd = ins
        out, igrad, d_a, d_o, d_1, d_2, r.smg, r.esg, r.tg = outs
        r.WH, r.W1 = [h0_, h1_], [w1a_, w1b_]
        r.x[...] = x_in[...]
        masks(r)
        near_bias(r)
        standardize_first(r)
        norm_first(r)
        project(r, 0)
        project(r, 1)

        over_pairs(attend_forward, r, 0, PAIRS, {})
        before_ff(r)

        def put_into(ref, step, first, wide):
            def put(i, value):
                rows = pl.ds(pl.multiple_of(i * step, step), step)
                ref[rows, first : first + wide] = value.astype(ref.dtype)

            return put

        for f in range(ff // WIDE):
            feed_forward(r, f)
        weight_grad(r.act, lambda: r.g[...], 1024, put_into(d_2, 1024, 0, D))
        for f in range(ff // WIDE):
            cols = slice(f * WIDE, (f + 1) * WIDE)
            feed_backward(r, f)
            weight_grad(
                r.nf, lambda cols=cols: r.gh[:, cols], D, put_into(d_1, D, f * WIDE, WIDE)
            )
        for i in range(length // BLOCK):
            after_ff(r, slice(i * BLOCK, (i + 1) * BLOCK))
        for i in range(length // BLOCK):
            output(r, slice(i * BLOCK, (i + 1) * BLOCK))
        out[...] = r.nf[...]
        weight_grad(r.att, lambda: r.gb[...], D, put_into(d_o, D, 0, D))
        over_pairs(attend_backward, r, 0, PAIRS, {})
        for half in range(2):
            back_project(r, half)

            def put(i, value, half=half):
                for part in range(3):
                    first = part * D + half * HALF
                    d_a[:, first : first + HALF] = value[
                        :, part * HALF : (part + 1) * HALF
                    ].astype(bf16)

            weight_grad(r.na, lambda half=half: r.gh[:, half_columns(half)], D, put)
        last(r)
        table_grad(r)
        igrad[...] = r.xh2[...]

    out_shape = [
        jax.ShapeDtypeStruct((length, D), bf16),
        jax.ShapeDtypeStruct((length, D), f32),
        jax.ShapeDtypeStruct((D, 3 * D), bf16),
        jax.ShapeDtypeStruct((D, D), bf16),
        jax.ShapeDtypeStruct((D, ff), bf16),
        jax.ShapeDtypeStruct((ff, D), bf16),
        jax.ShapeDtypeStruct((16, D), f32),
        jax.ShapeDtypeStruct((8, ff), f32),
        jax.ShapeDtypeStruct((HEADS, 128), f32),
    ]
    operands = [x, documents, g, h0, h1, w_o, w_1a, w_1b, w_2, sm, es, bd]
    return run_kernel(kernel, operands, out_shape, scratch)


def whole_body(dp_size, fsdp_size):
    def body(x, documents, fg, fs, w_a, table, w_o, os, sg, ss, w_1, es, w_2, rs, g):
        vectors = (fg, fs, os, sg, ss, rs, es, table)
        results = whole_layer(
            x,
            documents,
            g,
            [v.reshape(1, -1) for v in vectors],
            w_a,
            w_o,
            w_1,
            w_2,
            dp_size,
            fsdp_size,
        )
        out, igrad, d_a, d_o, d_1, d_2, *small = hand_out(
            results, [v.shape[0] for v in vectors]
        )
        dfg, dfs, dos, dsg, dss, drs, des, dtable = [v.reshape(-1) for v in small]
        return (out, igrad, dfg, dfs, d_a, dtable, d_o, dos, dsg, dss, d_1, des, d_2, drs)

    return body


def split_body(x, documents, fg, fs, w_a, table, w_o, os, sg, ss, w_1, es, w_2, rs, g):
    def whole(v):
        return lax.all_gather(v, AXES, axis=0, tiled=True)

    def mine(v):
        return lax.psum_scatter(v.astype(f32), AXES, scatter_dimension=0, tiled=True)

    parts = [w_a[:, i * HALF : (i + 1) * HALF] for i in range(6)]
    h0 = whole(jnp.concatenate(parts[0::2], axis=1))
    h1 = whole(jnp.concatenate(parts[1::2], axis=1))
    ff = w_1.shape[1]
    rows = [whole(v).astype(f32) for v in (fg, fs, os, sg, ss, rs)]
    sm = jnp.concatenate([jnp.stack(rows), jnp.zeros((10, D), f32)], axis=0)
    wide = jnp.tile(whole(es).astype(f32)[None], (8, 1))
    bias = whole(table).astype(f32).reshape(HEADS, BUCKETS)
    bd = bias[:, bucket_of(jnp.arange(256, dtype=jnp.int32))]
    w_1 = whole(w_1)
    out, igrad, d_a, d_o, d_1, d_2, smg, esg, tg = local_layer(
        x,
        documents,
        g,
        h0,
        h1,
        whole(w_o),
        w_1[:, : ff // 2],
        w_1[:, ff // 2 :],
        whole(w_2),
        sm,
        wide,
        bd,
    )
    return (
        out,
        igrad,
        mine(smg[0]),
        mine(smg[1]),
        mine(d_a),
        mine(tg[:, :BUCKETS].reshape(HEADS * BUCKETS)),
        mine(d_o),
        mine(smg[2]),
        mine(smg[3]),
        mine(smg[4]),
        mine(d_1),
        mine(esg[0]),
        mine(d_2),
        mine(smg[5]),
    )


def solution(mesh):
    rows, flat = P(AXES, None), P(AXES)
    dp_size, fsdp_size = mesh.shape["dp"], mesh.shape["fsdp"]
    one_kernel = (dp_size, fsdp_size) == (16, 2)
    return jax.shard_map(
        whole_body(dp_size, fsdp_size) if one_kernel else split_body,
        mesh=mesh,
        in_specs=(
            rows,
            rows,
            flat,
            flat,
            rows,
            flat,
            rows,
            flat,
            flat,
            flat,
            rows,
            flat,
            rows,
            flat,
            rows,
        ),
        out_specs=(rows, rows, flat, flat, rows, flat, rows, flat, flat, flat, rows, flat, rows, flat),
        check_vma=False,
    )
```
